128 devices in a mesh: row: 8 (over z, y_hi), col: 16 (over y_lo, x, core).
Axes of the slice: x: 4, y: 4 (y_hi: 2, y_lo: 2; y = y_hi * 2 + y_lo), z: 4, core: 2. Of those that a mesh axis runs over, the one named last changes fastest.
Arguments:
- col_data: bfloat16 [512, 4, 128, 128], P(('row', 'col')), may hold values from -0.029907227 to 0.029907227
- col_scale: bfloat16 [512, 128], P(('row', 'col')), may hold values from 0.0099487305 to 100
- row_ids: int32 [512, 4], P(('row', 'col')), may hold values from 0 to 31, as said below
- live_rows: int32 [512], P(('row', 'col')), may hold values from 1 to 4
- live_blocks: int32 [128], P(('row', 'col')), may hold values from 1 to 4, as said below
- row_reg: float32 [4096], replicated, may hold values from 0.05 to 0.5
Outputs:
- factored: float32 [4096, 4096], P('row', 'col')
The draws below stay inside these ranges and needn't reach their ends.
Inputs may be any that keep to these rules, and one draw needn't show every extreme that they name: row_ids[c, k] % 4 == k, and (row_ids[c, k] // 4) % 4 == (c % 4) % 4 for every column block c and slot k. `live_blocks`: one device has exactly 4 column blocks.
All inputs are finite; a program needn't handle non-finite values.
Results may differ from the reference program's by a relative error of at most 0.0003.
Values may be sent and summed in bfloat16 or wider, within the bound.
A program may use at most 128 MiB of HBM per device.

```python
import math
import jax
import jax.numpy as jnp
from jax import lax

B = 128
W = 128
ORDER = 4096
K = 4
PW = 512
CAP = 4
NB = 32
NBL = 4
NBC = 2
CBLK = 512
GRP = 4
N_ROW = 8
N_COL = 16


def draw_row_ids(key, part):
    key = jax.random.fold_in(key, 11)
    spread = NB // K // GRP
    base = jax.random.randint(key, (CBLK, K), 0, spread)
    classes = jnp.arange(CBLK) % CAP % GRP
    full = base * GRP + classes[:, None]
    return (full * K + jnp.arange(K)[None, :]).astype(jnp.int32)


def draw_live_blocks(key, part):
    key = jax.random.fold_in(key, 23)
    first, second = jax.random.split(key)
    count = CBLK // CAP
    values = jax.random.randint(first, (count,), 1, CAP + 1)
    chosen = jax.random.randint(second, (), 0, count)
    return values.at[chosen].set(CAP).astype(jnp.int32)


def with_ends(values, rng, low, high):
    longest = values.shape.index(max(values.shape))
    spots = []
    for shift in (0, 1):
        where = [jax.random.randint(jax.random.fold_in(rng, axis), (), 0, length) for axis, length in enumerate(values.shape)]
        where[longest] = (where[longest] + shift) % values.shape[longest]
        spots.append(tuple(where))
    return values.at[spots[0]].set(low).at[spots[1]].set(high)


def steps_of(own_key, dims, pieces, smallest, largest):
    def one(axis_at, blocks):
        steps = jax.random.uniform(jax.random.fold_in(jax.random.fold_in(own_key, 6), axis_at), (blocks,), jnp.float32, smallest / len(pieces), largest / len(pieces))
        return jnp.repeat(jnp.exp(steps), dims[axis_at] // blocks).reshape((-1,) + (1,) * (len(dims) - axis_at - 1))

    level = one(*pieces[0])
    for cut in pieces[1:]:
        level = level * one(*cut)
    return level


def centred(own_key, shape, scale, bound, cuts=(), held_as=jnp.bfloat16):
    values = jax.random.normal(own_key, shape, jnp.float32) * scale
    if len(cuts) > 0:
        values = steps_of(own_key, shape, cuts, -0.22, 0.18) * values
    return jnp.clip(values, min=-bound, max=bound).astype(held_as)


def setup_inputs(seed: int = 0) -> dict:
    seeds = jax.random.split(jax.random.key(seed), 7)
    return {
        "col_data": centred(seeds[0], (CBLK, K, B, W), 0.005, 0.029907227, ((0, 128),)),
        "col_scale": jnp.clip(jnp.exp(math.log(100.0) - 9.215481 * jax.random.uniform(seeds[1], (CBLK, W), jnp.float32) ** steps_of(seeds[1], (CBLK, W), ((0, 128),), -0.2, 0.2)), 0.0099487305, 100.0).astype(jnp.bfloat16),
        "row_ids": draw_row_ids(jax.random.fold_in(seeds[6], 71), 0),
        "live_rows": with_ends(jax.random.randint(seeds[3], (CBLK,), 1, K + 1), jax.random.fold_in(seeds[3], 1), 1, K).astype(jnp.int32),
        "live_blocks": draw_live_blocks(jax.random.fold_in(seeds[6], 71), 0),
        "row_reg": jnp.clip(jnp.exp(jax.random.uniform(seeds[5], (ORDER,), jnp.float32, math.log(0.05), math.log(0.5))), 0.05, 0.5),
    }


def reference(col_data, col_scale, row_ids, live_rows, live_blocks, row_reg):
    slot = jnp.arange(CBLK) % CAP
    device = jnp.arange(CBLK) // CAP
    slot_on = (slot < live_blocks[device]).astype(jnp.float32)
    piece_on = (jnp.arange(K)[None, :] < live_rows[:, None]).astype(jnp.float32)
    keep = slot_on[:, None] * piece_on
    data = (col_data.astype(jnp.float32) * keep[:, :, None, None]).astype(jnp.bfloat16)
    scaled = (data.astype(jnp.float32) * col_scale.astype(jnp.float32)[:, None, None, :]).astype(jnp.bfloat16)

    def add_group(total, group):
        start = (group * CAP).astype(jnp.int32)
        part_data = lax.dynamic_slice_in_dim(data, start, CAP, 0).astype(jnp.float32)
        part_scaled = lax.dynamic_slice_in_dim(scaled, start, CAP, 0).astype(jnp.float32)
        part_ids = lax.dynamic_slice_in_dim(row_ids, start, CAP, 0)
        product = jnp.einsum('nabw,ncdw->nacbd', part_scaled, part_data, precision=lax.Precision.HIGHEST)
        total = total.at[part_ids[:, :, None], part_ids[:, None, :]].add(product)
        return (total, None)
    groups = jnp.arange(CBLK // CAP, dtype=jnp.int32)
    blocks, unused = lax.scan(add_group, jnp.zeros((NB, NB, B, B), jnp.float32), groups)
    matrix = blocks.transpose(0, 2, 1, 3).reshape(ORDER, ORDER)
    diag_index = jnp.arange(ORDER, dtype=jnp.int32)
    matrix = matrix.at[diag_index, diag_index].add(row_reg)
    lower = jnp.linalg.cholesky(matrix[:PW, :PW])
    panel = jax.scipy.linalg.solve_triangular(lower, matrix[:, :PW].T, lower=True).T
    trailing = matrix[PW:, PW:] - jnp.dot(panel[PW:], panel[PW:].T, precision=lax.Precision.HIGHEST)
    result = jnp.zeros((ORDER, ORDER), jnp.float32)
    result = result.at[:, :PW].set(panel)
    result = result.at[PW:, PW:].set(trailing)
    grid = result.reshape(NB, B, NB, B)
    upos = jnp.arange(NB)
    row_sel = upos % NBL * N_ROW + upos // NBL
    col_sel = upos % NBC * N_COL + upos // NBC
    grid = grid[row_sel][:, :, col_sel]
    return grid.reshape(ORDER, ORDER)
```

```python
import jax, jax.numpy as jnp
from jax import lax
from jax.sharding import PartitionSpec as P
from jax.experimental import pallas as pl
from jax.experimental.pallas import tpu as pltpu

HI = lax.Precision.HIGHEST
NA = 896


def tdot(a, b):
    return lax.dot_general(a, b, (((0,), (0,)), ((), ())), precision=HI,
                           preferred_element_type=jnp.float32)


def bc(v):
    return jnp.broadcast_to(v, (8, 128))


def eliminate(x_ref):
    sub = lax.broadcasted_iota(jnp.int32, (8, 128), 0)
    for blk in range(4):
        lo = blk * 128
        nl = (NA - lo) // 128
        for h in range(4):
            r0 = lo + 32 * h
            xs = [[x_ref[r0 + 8 * b:r0 + 8 * b + 8, lo + 128 * l:lo + 128 * l + 128] for l in range(nl)]
                  for b in range(4)]
            for j in range(4):
                lane = 32 * h + 8 * j
                cs = {b: [bc(xs[b][0][:, lane + i:lane + i + 1]) for i in range(8)] for b in range(j, 4)}
                scale = jnp.zeros((8, 128), jnp.float32)
                for i in range(8):
                    p = bc(cs[j][i][i:i + 1, :])
                    rp = 1.0 / p
                    scale = jnp.where(sub == i, lax.rsqrt(p), scale)
                    f = {b: cs[b][i] * rp for b in range(j, 4)}
                    f[j] = jnp.where(sub > i, f[j], 0.0)
                    for m in range(i + 1, 8):
                        t = bc(cs[j][m][i:i + 1, :])
                        for b in range(j, 4):
                            cs[b][m] = cs[b][m] - f[b] * t
                    for l in range(nl):
                        t = bc(xs[j][l][i:i + 1, :])
                        for b in range(j, 4):
                            xs[b][l] = xs[b][l] - f[b] * t
                for l in range(nl):
                    xs[j][l] = xs[j][l] * scale
                    x_ref[r0 + 8 * j:r0 + 8 * j + 8, lo + 128 * l:lo + 128 * l + 128] = xs[j][l]
            if h < 3:
                u = x_ref[r0:r0 + 32, lo:NA]
                t = tdot(u[:, :128], u)
                x_ref[r0 + 32:lo + 128, lo:NA] = x_ref[r0 + 32:lo + 128, lo:NA] - t[32 * (h + 1):, :]
        for nxt in range(blk + 1, 4):
            c = nxt * 128
            x_ref[c:c + 128, c:NA] = x_ref[c:c + 128, c:NA] - tdot(
                x_ref[lo:lo + 128, c:c + 128], x_ref[lo:lo + 128, c:NA])


def kernel_c(panel, own, reg, out, x_ref):
    q = lax.axis_index("col")
    r = lax.axis_index("row")
    cls = q // 4
    kr = lax.rem(r, 4)
    kc = lax.rem(q, 4)
    owner = (r // 4) == lax.rem(cls, 2)
    eye = (lax.broadcasted_iota(jnp.int32, (128, 128), 0) == lax.broadcasted_iota(jnp.int32, (128, 128), 1))
    out[...] = jnp.zeros_like(out)

    def diag(block):
        return jnp.where(eye, jnp.broadcast_to(reg[pl.ds(block, 1), :], (128, 128)), 0.0)

    def blk(t, i, j):
        return jnp.concatenate([panel[0, t, i, j], panel[1, t, i, j]], axis=0)

    def mine(t, u):
        base = jnp.concatenate([own[t, u, 0], own[t, u, 1]], axis=0)
        if t == u:
            base = base + jnp.where(kr == kc, 1.0, 0.0) * diag(cls * 4 + kr + 16 * t)
        return base

    @pl.when(owner & (cls > 0))
    def _():
        for t in range(2):
            at = pl.multiple_of((cls // 2 + 2 * t) * 128, 128)
            for u in range(2):
                out[pl.ds(at, 128), u * 128:u * 128 + 128] = mine(t, u)

    @pl.when(owner & (cls == 0))
    def _():
        for i in range(4):
            for j in range(i, 4):
                s = 0.5 * (blk(0, i, j) + blk(0, j, i).T)
                if i == j:
                    s = s + diag(i)
                x_ref[i * 128:i * 128 + 128, j * 128:j * 128 + 128] = s
        for k in range(4):
            rows = slice(k * 128, k * 128 + 128)
            x_ref[rows, 512:640] = blk(0, kr, k).T + jnp.where(kr == k, 1.0, 0.0) * diag(k)
            x_ref[rows, 640:768] = blk(1, kr, k).T
            x_ref[rows, 768:896] = blk(1, kc, k).T
        eliminate(x_ref)
        at = pl.multiple_of(kc * 128, 128)
        out[0:128, 0:128] = x_ref[pl.ds(at, 128), 512:640].T
        out[256:384, 0:128] = x_ref[pl.ds(at, 128), 640:768].T
        out[256:384, 128:256] = mine(1, 1) - tdot(x_ref[:, 640:768], x_ref[:, 768:896])


def finish(panel, own, reg):
    return pl.pallas_call(
        kernel_c,
        out_shape=jax.ShapeDtypeStruct((512, 256), jnp.float32),
        in_specs=[pl.BlockSpec(memory_space=pltpu.VMEM)] * 3,
        out_specs=pl.BlockSpec(memory_space=pltpu.VMEM),
        scratch_shapes=[pltpu.VMEM((512, NA), jnp.float32)],
        compiler_params=pltpu.CompilerParams(vmem_limit_bytes=40 * 1024 * 1024),
    )(panel, own, reg)
ROWS = 528
MESH = pl.DeviceIdType.MESH


def kernel_a(data, scale, ids, live_rows, live_blocks, own, panel,
             gat, lbuf, rbuf, part, land, res,
             w1s, w1f, w1r, w2s, w2r, w3s, panel_r, own_r, sib_s, sib_r):
    r = lax.axis_index("row")
    q = lax.axis_index("col")
    z, yh = r // 2, lax.rem(r, 2)
    zh, zl = z // 2, lax.rem(z, 2)
    yl, j = q // 8, lax.rem(q, 8)
    x, e = j // 2, lax.rem(j, 2)
    xh, xl = x // 2, lax.rem(x, 2)
    pos = 2 * r + yl
    cls = 2 * yl + xh
    sibling = (r, q + 1 - 2 * e)

    def ring(d):
        x2 = lax.rem(x + d, 4)
        return (r, yl * 8 + 2 * x2 + e), 2 * x2 + e

    def plane(p):
        return (p // 2, lax.rem(p, 2) * 8 + j)

    barrier = pltpu.get_barrier_semaphore()
    for d in range(1, 4):
        pl.semaphore_signal(barrier, inc=1, device_id=ring(d)[0], device_id_type=MESH)
    pl.semaphore_signal(barrier, inc=1, device_id=sibling, device_id_type=MESH)
    for d in range(1, 16):
        pl.semaphore_signal(barrier, inc=1, device_id=plane(lax.rem(pos + d, 16)), device_id_type=MESH)

    def prepare(s):
        row = lax.broadcasted_iota(jnp.int32, (16, 128), 0)
        on = s < live_blocks[0]
        meta = jnp.where(row == 0, jnp.broadcast_to(scale[...].astype(jnp.float32)[s:s + 1, :], (16, 128)), 0.0)
        for k in range(4):
            keep = jnp.where(on & (k < live_rows[s]), 1.0, 0.0)
            gat[s, j, k * 128:k * 128 + 128, :] = (data[s, k].astype(jnp.float32) * keep).astype(jnp.bfloat16)
            late = jnp.where(ids[s, k] >= 16, 1.0, 0.0)
            meta = jnp.where(row == k + 1, late, meta)
        gat[s, j, 512:528, :] = meta.astype(jnp.bfloat16)

    def w1_copy(s, d):
        target = sibling if d == 0 else ring(d)[0]
        return pltpu.make_async_remote_copy(
            src_ref=gat.at[s, j], dst_ref=gat.at[s, j], send_sem=w1s.at[s, d], recv_sem=w1r.at[s, j],
            device_id=target, device_id_type=MESH)

    def forward_copy(s, d):
        j2 = ring(d)[1]
        return pltpu.make_async_remote_copy(
            src_ref=gat.at[s, j2], dst_ref=gat.at[s, j2], send_sem=w1f.at[s, d - 1], recv_sem=w1r.at[s, j2],
            device_id=sibling, device_id_type=MESH)

    def w1_arrived(s, j2):
        pltpu.make_async_remote_copy(
            src_ref=gat.at[s, j2], dst_ref=gat.at[s, j2], send_sem=w1f.at[s, 0], recv_sem=w1r.at[s, j2],
            device_id=sibling, device_id_type=MESH).wait_recv()

    def w2_copy(s, d):
        to = lax.rem(pos + d, 16)
        return pltpu.make_async_remote_copy(
            src_ref=part.at[s, to], dst_ref=land.at[s, pos], send_sem=w2s.at[s, d - 1], recv_sem=w2r.at[s, pos],
            device_id=plane(to), device_id_type=MESH)

    def w2_arrived(s, src):
        pltpu.make_async_remote_copy(
            src_ref=part.at[s, src], dst_ref=land.at[s, src], send_sem=w2s.at[s, 0], recv_sem=w2r.at[s, src],
            device_id=plane(src), device_id_type=MESH).wait_recv()

    def forward(s):
        for d in (1, 3, 2):
            w1_arrived(s, ring(d)[1])
            forward_copy(s, d).start()

    def compute(s):
        w1_arrived(s, 2 * x + 1 - e)
        for d in (1, 3, 2):
            w1_arrived(s, 2 * lax.rem(x + d, 4) + 1 - e)

        def build(c, _):
            meta = gat[s, c, 512:528, :].astype(jnp.float32)
            sc = meta[0:1, :]
            at = pl.multiple_of(c * 128, 128)
            for k in range(2):
                t = jnp.where(xh == 0, meta[1 + k:2 + k, :], meta[3 + k:4 + k, :])
                a = gat[s, c, pl.ds(pl.multiple_of((2 * xh + k) * 128, 128), 128), :].astype(jnp.float32)
                g = (a * sc).astype(jnp.bfloat16).astype(jnp.float32)
                lbuf[2 * k * 128:2 * k * 128 + 128, pl.ds(at, 128)] = (g * (1.0 - t)).astype(jnp.bfloat16)
                lbuf[2 * k * 128 + 128:2 * k * 128 + 256, pl.ds(at, 128)] = (g * t).astype(jnp.bfloat16)
            t0 = jnp.where(e == 0, meta[1:2, :], meta[2:3, :])
            t1 = jnp.where(e == 0, meta[3:4, :], meta[4:5, :])
            t = jnp.where(xl == 0, t0, t1)
            a = gat[s, c, pl.ds(pl.multiple_of((2 * xl + e) * 128, 128), 128), :].astype(jnp.float32)
            rbuf[0:128, pl.ds(at, 128)] = (a * (1.0 - t)).astype(jnp.bfloat16)
            rbuf[128:256, pl.ds(at, 128)] = (a * t).astype(jnp.bfloat16)
            return 0

        lax.fori_loop(0, 8, build, 0)
        for k in range(2):
            for t in range(2):
                row = (2 * k + t) * 128
                acc = lax.dot_general(lbuf[row:row + 128, :], rbuf[...], (((1,), (1,)), ((), ())),
                                      preferred_element_type=jnp.float32)
                for half in range(2):
                    for u in range(2):
                        part[s, t * 8 + half * 4 + k * 2 + u] = acc[half * 64:half * 64 + 64, u * 128:u * 128 + 128]

    def panel_copy(d):
        xd, yd, zd = d % 2, (d // 2) % 2, d // 4
        to = (zd * 2 + yd, xd * 2 + zl)
        kr, kc = 2 * xh + yh, 2 * xl + e
        copy = pltpu.make_async_remote_copy(
            src_ref=res.at[0], dst_ref=panel.at[zl, zh, kr, kc], send_sem=w3s.at[0, d],
            recv_sem=panel_r.at[zh, kr, kc], device_id=to, device_id_type=MESH)
        return copy, (to[0] != r) | (to[1] != q)

    def own_copy(s):
        sh, sl = s // 2, lax.rem(s, 2)
        to = ((2 * sl + xh) * 2 + yh, sh * 8 + (2 * sl + xl) * 2 + e)
        copy = pltpu.make_async_remote_copy(
            src_ref=res.at[s], dst_ref=own.at[zh, yl, zl], send_sem=w3s.at[s, 0],
            recv_sem=own_r.at[zh, yl, zl], device_id=to, device_id_type=MESH)
        return copy, (to[0] != r) | (to[1] != q)

    def finish_sum(s):
        for d in range(1, 16):
            w2_arrived(s, lax.rem(pos + d, 16))
        total = part[s, pos]
        for d in range(1, 16):
            total = total + land[s, lax.rem(pos + d, 16)]
        res[s] = total

        @pl.when(s == 0)
        def _():
            @pl.when(yl == 0)
            def _():
                for d in range(8):
                    copy, remote = panel_copy(d)
                    pl.when(remote)(copy.start)

                @pl.when((cls == 0) & (zh == 0) & (zl == e))
                def _():
                    panel[zl, 0, yh, 2 * xl + e] = total

            @pl.when((yl == 1) & (zh == 1))
            def _():
                own_copy(s)[0].start()

        @pl.when(s > 0)
        def _():
            copy, remote = own_copy(s)
            pl.when(remote)(copy.start)

            @pl.when(jnp.logical_not(remote))
            def _():
                own[zh, yl, zl] = total

    prepare(0)
    pl.semaphore_wait(barrier, 19)
    for d in (1, 3, 2, 0):
        w1_copy(0, d).start()

    for s in range(1, 4):
        prepare(s)
        for d in (1, 3, 2, 0):
            w1_copy(s, d).start()
    forward(0)

    def step(s, _):
        compute(s)
        for d in range(1, 16):
            w2_copy(s, d).start()

        @pl.when(s < 3)
        def _():
            forward(s + 1)

        finish_sum(s)
        return 0

    lax.fori_loop(0, 4, step, 0)

    @pl.when((cls == 0) & (zh == 0))
    def _():
        for t in range(2):
            def arrived(i, _):
                a, b = i // 4, lax.rem(i, 4)
                here = (t == 0) & (a == yh) & (b == 2 * xl + e) & (zl == e)

                @pl.when(jnp.logical_not(here))
                def _():
                    pltpu.make_async_remote_copy(
                        src_ref=res.at[0], dst_ref=panel.at[e, t, a, b], send_sem=w3s.at[0, 0],
                        recv_sem=panel_r.at[t, a, b], device_id=sibling, device_id_type=MESH).wait_recv()
                return 0

            lax.fori_loop(0, 16, arrived, 0)
            pltpu.make_async_remote_copy(
                src_ref=panel.at[e, t], dst_ref=panel.at[e, t], send_sem=sib_s.at[t], recv_sem=sib_r.at[t],
                device_id=sibling, device_id_type=MESH).start()
        for t in range(2):
            copy = pltpu.make_async_remote_copy(
                src_ref=panel.at[e, t], dst_ref=panel.at[1 - e, t], send_sem=sib_s.at[t], recv_sem=sib_r.at[t],
                device_id=sibling, device_id_type=MESH)
            copy.wait_recv()
            copy.wait_send()

    @pl.when(zh == xh)
    def _():
        for t in range(2):
            for u in range(2):
                for half in range(2):
                    here = (xh == zl) & (yl == u) & (zh == t) & (zl == half)
                    wanted = ((cls > 0) & jnp.logical_not(here)) | ((cls == 0) & (t == 1) & (u == 1))

                    @pl.when(wanted)
                    def _():
                        pltpu.make_async_remote_copy(
                            src_ref=res.at[0], dst_ref=own.at[t, u, half], send_sem=w3s.at[0, 0],
                            recv_sem=own_r.at[t, u, half], device_id=sibling, device_id_type=MESH).wait_recv()

    def sent(s, _):
        for d in range(4):
            w1_copy(s, d).wait_send()
        for d in range(1, 4):
            forward_copy(s, d).wait_send()
        for d in range(1, 16):
            w2_copy(s, d).wait_send()

        @pl.when(s > 0)
        def _():
            copy, remote = own_copy(s)
            pl.when(remote)(copy.wait_send)
        return 0

    lax.fori_loop(0, 4, sent, 0)

    @pl.when(yl == 0)
    def _():
        for d in range(8):
            copy, remote = panel_copy(d)
            pl.when(remote)(copy.wait_send)

    @pl.when((yl == 1) & (zh == 1))
    def _():
        own_copy(0)[0].wait_send()


def assemble(data, scale, ids, live_rows, live_blocks):
    vmem = pl.BlockSpec(memory_space=pltpu.VMEM)
    smem = pl.BlockSpec(memory_space=pltpu.SMEM)
    dma = pltpu.SemaphoreType.DMA
    return pl.pallas_call(
        kernel_a,
        out_shape=(jax.ShapeDtypeStruct((2, 2, 2, 64, 128), jnp.float32),
                   jax.ShapeDtypeStruct((2, 2, 4, 4, 64, 128), jnp.float32)),
        in_specs=[vmem, vmem, smem, smem, smem],
        out_specs=(vmem, vmem),
        scratch_shapes=[
            pltpu.VMEM((4, 8, ROWS, 128), jnp.bfloat16),
            pltpu.VMEM((512, 1024), jnp.bfloat16),
            pltpu.VMEM((256, 1024), jnp.bfloat16),
            pltpu.VMEM((4, 16, 64, 128), jnp.float32),
            pltpu.VMEM((4, 16, 64, 128), jnp.float32),
            pltpu.VMEM((4, 64, 128), jnp.float32),
            dma((4, 4)), dma((4, 3)), dma((4, 8)), dma((4, 15)), dma((4, 16)), dma((4, 8)),
            dma((2, 4, 4)), dma((2, 2, 2)), dma((2,)), dma((2,)),
        ],
        compiler_params=pltpu.CompilerParams(
            collective_id=0, has_side_effects=True, vmem_limit_bytes=40 * 1024 * 1024),
    )(data, scale, ids, live_rows, live_blocks)


def body(col_data, col_scale, row_ids, live_rows, live_blocks, row_reg):
    own, panel = assemble(col_data, col_scale, row_ids, live_rows, live_blocks)
    return finish(panel, own, row_reg.reshape(32, 128))


def solution(mesh):
    return jax.shard_map(
        body,
        mesh=mesh,
        in_specs=(
            P(("row", "col"), None, None, None),
            P(("row", "col"), None),
            P(("row", "col"), None),
            P(("row", "col")),
            P(("row", "col")),
            P(),
        ),
        out_specs=P("row", "col"),
        check_vma=False,
    )
```

```python
import jax
import jax.numpy as jnp
from jax import lax
from jax.experimental import pallas as pl
from jax.experimental.pallas import tpu as pltpu
from jax.sharding import PartitionSpec as P

HI = lax.Precision.HIGHEST
NA = 896
ROWS = 528
MESH = pl.DeviceIdType.MESH


def tdot(a, b):
    return lax.dot_general(a, b, (((0,), (0,)), ((), ())), precision=HI,
                           preferred_element_type=jnp.float32)


def fdot(a, b):
    return jnp.dot(a, b, precision=HI, preferred_element_type=jnp.float32)


def lanes(v):
    return jnp.broadcast_to(v, (v.shape[0], 128))


def diag_factor(d, between=None):
    row8 = lax.broadcasted_iota(jnp.int32, (8, 128), 0)
    e = jnp.where(lax.broadcasted_iota(jnp.int32, (128, 128), 0) == lax.broadcasted_iota(jnp.int32, (128, 128), 1), 1.0, 0.0)
    us, es = [], []
    for h in range(4):
        x, y = d[:32], e[:32]
        done_x, done_y = [], []
        for j in range(4):
            lane = 32 * h + 8 * j
            rows = 32 - 8 * j
            row = lax.broadcasted_iota(jnp.int32, (rows, 128), 0)
            cs = [lanes(x[:, lane + i:lane + i + 1]) for i in range(8)]
            scale = jnp.zeros((8, 128), jnp.float32)
            for i in range(8):
                p = cs[i][i:i + 1, :]
                rp = 1.0 / p
                scale = jnp.where(row8 == i, lax.rsqrt(p), scale)
                f = jnp.where(row > i, cs[i] * rp, 0.0)
                for m in range(i + 1, 8):
                    cs[m] = cs[m] - f * cs[m][i:i + 1, :]
                x = x - f * x[i:i + 1, :]
                y = y - f * y[i:i + 1, :]
            done_x.append(x[:8] * scale)
            done_y.append(y[:8] * scale)
            x, y = x[8:], y[8:]
        ux = jnp.concatenate(done_x, axis=0)
        uy = jnp.concatenate(done_y, axis=0)
        us.append(ux)
        es.append(uy)
        if h < 3:
            n = 128 - 32 * (h + 1)
            left = ux[:, :]
            d = d[32:] - tdot(left, ux)[32 * (h + 1):]
            e = e[32:] - tdot(left, uy)[32 * (h + 1):]
    return jnp.concatenate(us, axis=0), jnp.concatenate(es, axis=0)


def kernel(data_h, scale_h, ids_h, live_rows_h, live_blocks_h, reg_h, out,
           data, scale, ids, live_rows, live_blocks, reg, own, panel,
           gat, lbuf, rbuf, part, land, res, x_ref,
           ins, w1s, w1f, w1r, w2s, w2r, w3s, panel_r, own_r, sib_s, sib_r):
    loads = [pltpu.make_async_copy(a, b, ins.at[i]) for i, (a, b) in enumerate((
        (ids_h, ids), (live_rows_h, live_rows), (live_blocks_h, live_blocks), (scale_h, scale),
        (data_h.at[0], data.at[0]), (data_h.at[1], data.at[1]), (data_h.at[2], data.at[2]),
        (data_h.at[3], data.at[3]), (reg_h, reg)))]
    for load in loads:
        load.start()
    r = lax.axis_index("row")
    q = lax.axis_index("col")
    z, yh = r // 2, lax.rem(r, 2)
    zh, zl = z // 2, lax.rem(z, 2)
    yl, j = q // 8, lax.rem(q, 8)
    x, e = j // 2, lax.rem(j, 2)
    xh, xl = x // 2, lax.rem(x, 2)
    pos = 2 * r + yl
    cls = 2 * yl + xh
    sibling = (r, q + 1 - 2 * e)

    def ring(d):
        x2 = lax.rem(x + d, 4)
        return (r, yl * 8 + 2 * x2 + e), 2 * x2 + e

    def plane(p):
        return (p // 2, lax.rem(p, 2) * 8 + j)

    barrier = pltpu.get_barrier_semaphore()
    for d in range(1, 4):
        pl.semaphore_signal(barrier, inc=1, device_id=ring(d)[0], device_id_type=MESH)
    pl.semaphore_signal(barrier, inc=1, device_id=sibling, device_id_type=MESH)
    for d in range(1, 16):
        pl.semaphore_signal(barrier, inc=1, device_id=plane(lax.rem(pos + d, 16)), device_id_type=MESH)

    def prepare(s):
        row = lax.broadcasted_iota(jnp.int32, (16, 128), 0)
        on = s < live_blocks[0]
        meta = jnp.where(row == 0, jnp.broadcast_to(scale[...].astype(jnp.float32)[s:s + 1, :], (16, 128)), 0.0)
        for k in range(4):
            keep = jnp.where(on & (k < live_rows[s]), 1.0, 0.0)
            gat[s, j, k * 128:k * 128 + 128, :] = (data[s, k].astype(jnp.float32) * keep).astype(jnp.bfloat16)
            late = jnp.where(ids[s, k] >= 16, 1.0, 0.0)
            meta = jnp.where(row == k + 1, late, meta)
        gat[s, j, 512:528, :] = meta.astype(jnp.bfloat16)

    def w1_copy(s, d):
        target = sibling if d == 0 else ring(d)[0]
        return pltpu.make_async_remote_copy(
            src_ref=gat.at[s, j], dst_ref=gat.at[s, j], send_sem=w1s.at[s, d], recv_sem=w1r.at[s, j],
            device_id=target, device_id_type=MESH)

    def forward_copy(s, d):
        j2 = ring(d)[1]
        return pltpu.make_async_remote_copy(
            src_ref=gat.at[s, j2], dst_ref=gat.at[s, j2], send_sem=w1f.at[s, d - 1], recv_sem=w1r.at[s, j2],
            device_id=sibling, device_id_type=MESH)

    def w1_arrived(s, j2):
        pltpu.make_async_remote_copy(
            src_ref=gat.at[s, j2], dst_ref=gat.at[s, j2], send_sem=w1f.at[s, 0], recv_sem=w1r.at[s, j2],
            device_id=sibling, device_id_type=MESH).wait_recv()

    def w2_copy(s, d):
        to = lax.rem(pos + d, 16)
        return pltpu.make_async_remote_copy(
            src_ref=part.at[s, to], dst_ref=land.at[s, pos], send_sem=w2s.at[s, d - 1], recv_sem=w2r.at[s, pos],
            device_id=plane(to), device_id_type=MESH)

    def w2_arrived(s, src):
        pltpu.make_async_remote_copy(
            src_ref=part.at[s, src], dst_ref=land.at[s, src], send_sem=w2s.at[s, 0], recv_sem=w2r.at[s, src],
            device_id=plane(src), device_id_type=MESH).wait_recv()

    def forward(s):
        for d in (1, 3, 2):
            w1_arrived(s, ring(d)[1])
            forward_copy(s, d).start()

    def compute(s):
        w1_arrived(s, 2 * x + 1 - e)
        for d in (1, 3, 2):
            w1_arrived(s, 2 * lax.rem(x + d, 4) + 1 - e)

        def build(c, _):
            meta = gat[s, c, 512:528, :].astype(jnp.float32)
            sc = meta[0:1, :]
            at = pl.multiple_of(c * 128, 128)
            for k in range(2):
                t = jnp.where(xh == 0, meta[1 + k:2 + k, :], meta[3 + k:4 + k, :])
                a = gat[s, c, pl.ds(pl.multiple_of((2 * xh + k) * 128, 128), 128), :].astype(jnp.float32)
                g = (a * sc).astype(jnp.bfloat16).astype(jnp.float32)
                lbuf[2 * k * 128:2 * k * 128 + 128, pl.ds(at, 128)] = (g * (1.0 - t)).astype(jnp.bfloat16)
                lbuf[2 * k * 128 + 128:2 * k * 128 + 256, pl.ds(at, 128)] = (g * t).astype(jnp.bfloat16)
            t0 = jnp.where(e == 0, meta[1:2, :], meta[2:3, :])
            t1 = jnp.where(e == 0, meta[3:4, :], meta[4:5, :])
            t = jnp.where(xl == 0, t0, t1)
            a = gat[s, c, pl.ds(pl.multiple_of((2 * xl + e) * 128, 128), 128), :].astype(jnp.float32)
            rbuf[0:128, pl.ds(at, 128)] = (a * (1.0 - t)).astype(jnp.bfloat16)
            rbuf[128:256, pl.ds(at, 128)] = (a * t).astype(jnp.bfloat16)
            return 0

        lax.fori_loop(0, 8, build, 0)
        for k in range(2):
            for t in range(2):
                row = (2 * k + t) * 128
                acc = lax.dot_general(lbuf[row:row + 128, :], rbuf[...], (((1,), (1,)), ((), ())),
                                      preferred_element_type=jnp.float32)
                for half in range(2):
                    for u in range(2):
                        part[s, t * 8 + half * 4 + k * 2 + u] = acc[half * 64:half * 64 + 64, u * 128:u * 128 + 128]

    def panel_copy(d):
        xd, yd, zd = d % 2, (d // 2) % 2, d // 4
        to = (zd * 2 + yd, xd * 2 + zl)
        kr, kc = 2 * xh + yh, 2 * xl + e
        copy = pltpu.make_async_remote_copy(
            src_ref=res.at[0], dst_ref=panel.at[zl, zh, kr, kc], send_sem=w3s.at[0, d],
            recv_sem=panel_r.at[zh, kr, kc], device_id=to, device_id_type=MESH)
        return copy, (to[0] != r) | (to[1] != q)

    def own_copy(s):
        sh, sl = s // 2, lax.rem(s, 2)
        to = ((2 * sl + xh) * 2 + yh, sh * 8 + (2 * sl + xl) * 2 + e)
        copy = pltpu.make_async_remote_copy(
            src_ref=res.at[s], dst_ref=own.at[zh, yl, zl], send_sem=w3s.at[s, 0],
            recv_sem=own_r.at[zh, yl, zl], device_id=to, device_id_type=MESH)
        return copy, (to[0] != r) | (to[1] != q)

    def finish_sum(s):
        for d in range(1, 16):
            w2_arrived(s, lax.rem(pos + d, 16))
        total = part[s, pos]
        for d in range(1, 16):
            total = total + land[s, lax.rem(pos + d, 16)]
        res[s] = total

        @pl.when(s == 0)
        def _():
            @pl.when(yl == 0)
            def _():
                for d in range(8):
                    copy, remote = panel_copy(d)
                    pl.when(remote)(copy.start)

                @pl.when((cls == 0) & (zh == 0) & (zl == e))
                def _():
                    panel[zl, 0, yh, 2 * xl + e] = total

            @pl.when((yl == 1) & (zh == 1))
            def _():
                own_copy(s)[0].start()

        @pl.when(s > 0)
        def _():
            copy, remote = own_copy(s)
            pl.when(remote)(copy.start)

            @pl.when(jnp.logical_not(remote))
            def _():
                own[zh, yl, zl] = total

    eye = (lax.broadcasted_iota(jnp.int32, (128, 128), 0) == lax.broadcasted_iota(jnp.int32, (128, 128), 1))
    kr, kc = lax.rem(r, 4), lax.rem(q, 4)

    def diag(block):
        return jnp.where(eye, jnp.broadcast_to(reg[pl.ds(block, 1), :], (128, 128)), 0.0)

    def blk(t, a, b):
        return jnp.concatenate([panel[0, t, a, b], panel[1, t, a, b]], axis=0)

    def mine(t, u):
        base = jnp.concatenate([own[t, u, 0], own[t, u, 1]], axis=0)
        if t == u:
            base = base + jnp.where(kr == kc, 1.0, 0.0) * diag(cls * 4 + kr + 16 * t)
        return base

    def panel_half(t):
        def arrived(i, _):
            a, b = i // 4, lax.rem(i, 4)
            here = (t == 0) & (a == yh) & (b == 2 * xl + e) & (zl == e)

            @pl.when(jnp.logical_not(here))
            def _():
                pltpu.make_async_remote_copy(
                    src_ref=res.at[0], dst_ref=panel.at[e, t, a, b], send_sem=w3s.at[0, 0],
                    recv_sem=panel_r.at[t, a, b], device_id=sibling, device_id_type=MESH).wait_recv()
            return 0

        lax.fori_loop(0, 16, arrived, 0)
        pltpu.make_async_remote_copy(
            src_ref=panel.at[e, t], dst_ref=panel.at[e, t], send_sem=sib_s.at[t], recv_sem=sib_r.at[t],
            device_id=sibling, device_id_type=MESH).start()

    def panel_rest(t):
        copy = pltpu.make_async_remote_copy(
            src_ref=panel.at[e, t], dst_ref=panel.at[1 - e, t], send_sem=sib_s.at[t], recv_sem=sib_r.at[t],
            device_id=sibling, device_id_type=MESH)
        copy.wait_recv()
        copy.wait_send()

    def own_wait(t, u, half):
        pltpu.make_async_remote_copy(
            src_ref=res.at[0], dst_ref=own.at[t, u, half], send_sem=w3s.at[0, 0],
            recv_sem=own_r.at[t, u, half], device_id=sibling, device_id_type=MESH).wait_recv()

    def factor():
        panel_half(0)
        panel_rest(0)
        for i in range(4):
            for k in range(i, 4):
                s = 0.5 * (blk(0, i, k) + blk(0, k, i).T)
                if i == k:
                    s = s + diag(i)
                x_ref[i * 128:i * 128 + 128, k * 128:k * 128 + 128] = s
            x_ref[i * 128:i * 128 + 128, 512:640] = blk(0, kr, i).T + jnp.where(kr == i, 1.0, 0.0) * diag(i)
        first = None
        for n in range(4):
            lo, hi = n * 128, n * 128 + 128
            width = 640 if n == 0 else NA
            ud, li = diag_factor(x_ref[lo:hi, lo:hi])
            if n == 0:
                first = li
                panel_half(1)
            if n == 1:
                panel_rest(1)
                for k in range(4):
                    x_ref[k * 128:k * 128 + 128, 640:768] = blk(1, kr, k).T
                    x_ref[k * 128:k * 128 + 128, 768:896] = blk(1, kc, k).T
                u = fdot(first, x_ref[0:128, 640:NA])
                x_ref[0:128, 640:NA] = u
                x_ref[128:512, 640:NA] = x_ref[128:512, 640:NA] - tdot(x_ref[0:128, 128:512], u)
            u = fdot(li, x_ref[lo:hi, hi:width])
            x_ref[lo:hi, hi:width] = u
            for nxt in range(n + 1, 4):
                c = nxt * 128
                x_ref[c:c + 128, c:width] = x_ref[c:c + 128, c:width] - tdot(u[:, c - hi:c - hi + 128], u[:, c - hi:])
            if n == 2:
                finish_sum(1)
            if n == 3:
                finish_sum(2)
                finish_sum(3)
        at = pl.multiple_of(kc * 128, 128)
        out[0:128, 0:128] = x_ref[pl.ds(at, 128), 512:640].T
        out[256:384, 0:128] = x_ref[pl.ds(at, 128), 640:768].T
        left = tdot(x_ref[:, 640:768], x_ref[:, 768:896])
        for half in range(2):
            own_wait(1, 1, half)
        out[256:384, 128:256] = mine(1, 1) - left

    def send_w1(s):
        for d in (1, 3, 2, 0):
            w1_copy(s, d).start()

    def send_w2(s):
        for d in range(1, 16):
            w2_copy(s, d).start()

    for i in range(5):
        loads[i].wait()
    prepare(0)
    pl.semaphore_wait(barrier, 19)
    send_w1(0)
    for s in range(1, 4):
        loads[s + 4].wait()
        prepare(s)
    loads[8].wait()
    out[...] = jnp.zeros_like(out)
    forward(0)
    send_w1(1)
    compute(0)
    send_w2(0)
    forward(1)
    send_w1(2)
    finish_sum(0)
    compute(1)
    send_w2(1)
    forward(2)
    send_w1(3)
    compute(2)
    send_w2(2)
    forward(3)
    compute(3)
    send_w2(3)

    first_owner = (cls == 0) & (zh == 0)
    pl.when(first_owner)(factor)

    @pl.when(jnp.logical_not(first_owner))
    def _():
        for s in range(1, 4):
            finish_sum(s)

    @pl.when((cls > 0) & (zh == xh))
    def _():
        for t in range(2):
            for u in range(2):
                for half in range(2):
                    here = (xh == zl) & (yl == u) & (zh == t) & (zl == half)
                    pl.when(jnp.logical_not(here))(lambda t=t, u=u, half=half: own_wait(t, u, half))
        for t in range(2):
            at = pl.multiple_of((cls // 2 + 2 * t) * 128, 128)
            for u in range(2):
                out[pl.ds(at, 128), u * 128:u * 128 + 128] = mine(t, u)

    def sent(s, _):
        for d in range(4):
            w1_copy(s, d).wait_send()
        for d in range(1, 4):
            forward_copy(s, d).wait_send()
        for d in range(1, 16):
            w2_copy(s, d).wait_send()

        @pl.when(s > 0)
        def _():
            copy, remote = own_copy(s)
            pl.when(remote)(copy.wait_send)
        return 0

    lax.fori_loop(0, 4, sent, 0)

    @pl.when(yl == 0)
    def _():
        for d in range(8):
            copy, remote = panel_copy(d)
            pl.when(remote)(copy.wait_send)

    @pl.when((yl == 1) & (zh == 1))
    def _():
        own_copy(0)[0].wait_send()


def body(col_data, col_scale, row_ids, live_rows, live_blocks, row_reg):
    anywhere = pl.BlockSpec(memory_space=pl.ANY)
    dma = pltpu.SemaphoreType.DMA
    return pl.pallas_call(
        kernel,
        out_shape=jax.ShapeDtypeStruct((512, 256), jnp.float32),
        in_specs=[anywhere] * 6,
        out_specs=pl.BlockSpec(memory_space=pltpu.VMEM),
        scratch_shapes=[
            pltpu.VMEM((4, 4, 128, 128), jnp.bfloat16),
            pltpu.VMEM((4, 128), jnp.bfloat16),
            pltpu.SMEM((4, 4), jnp.int32),
            pltpu.SMEM((4,), jnp.int32),
            pltpu.SMEM((1,), jnp.int32),
            pltpu.VMEM((32, 128), jnp.float32),
            pltpu.VMEM((2, 2, 2, 64, 128), jnp.float32),
            pltpu.VMEM((2, 2, 4, 4, 64, 128), jnp.float32),
            pltpu.VMEM((4, 8, ROWS, 128), jnp.bfloat16),
            pltpu.VMEM((512, 1024), jnp.bfloat16),
            pltpu.VMEM((256, 1024), jnp.bfloat16),
            pltpu.VMEM((4, 16, 64, 128), jnp.float32),
            pltpu.VMEM((4, 16, 64, 128), jnp.float32),
            pltpu.VMEM((4, 64, 128), jnp.float32),
            pltpu.VMEM((512, NA), jnp.float32),
            dma((9,)),
            dma((4, 4)), dma((4, 3)), dma((4, 8)), dma((4, 15)), dma((4, 16)), dma((4, 8)),
            dma((2, 4, 4)), dma((2, 2, 2)), dma((2,)), dma((2,)),
        ],
        compiler_params=pltpu.CompilerParams(
            collective_id=0, has_side_effects=True, vmem_limit_bytes=60 * 1024 * 1024),
    )(col_data, col_scale, row_ids, live_rows, live_blocks, row_reg.reshape(32, 128))


def solution(mesh):
    return jax.shard_map(
        body,
        mesh=mesh,
        in_specs=(
            P(("row", "col"), None, None, None),
            P(("row", "col"), None),
            P(("row", "col"), None),
            P(("row", "col")),
            P(("row", "col")),
            P(),
        ),
        out_specs=P("row", "col"),
        check_vma=False,
    )
```

```python
import jax
import jax.numpy as jnp
from jax import lax
from jax.experimental import pallas as pl
from jax.experimental.pallas import tpu as pltpu
from jax.sharding import PartitionSpec as P

HI = lax.Precision.HIGHEST
NA = 896
ROWS = 528
MESH = pl.DeviceIdType.MESH


def tdot(a, b):
    return lax.dot_general(a, b, (((0,), (0,)), ((), ())), precision=HI,
                           preferred_element_type=jnp.float32)


def fdot(a, b):
    return jnp.dot(a, b, precision=HI, preferred_element_type=jnp.float32)


def lanes(v):
    return jnp.broadcast_to(v, (v.shape[0], 128))


def diag_factor(d, between=None):
    row8 = lax.broadcasted_iota(jnp.int32, (8, 128), 0)
    e = jnp.where(lax.broadcasted_iota(jnp.int32, (128, 128), 0) == lax.broadcasted_iota(jnp.int32, (128, 128), 1), 1.0, 0.0)
    us, es = [], []
    for h in range(4):
        x, y = d[:32], e[:32]
        done_x, done_y = [], []
        for j in range(4):
            lane = 32 * h + 8 * j
            rows = 32 - 8 * j
            row = lax.broadcasted_iota(jnp.int32, (rows, 128), 0)
            cs = [lanes(x[:, lane + i:lane + i + 1]) for i in range(8)]
            scale = jnp.zeros((8, 128), jnp.float32)
            for i in range(8):
                p = cs[i][i:i + 1, :]
                rp = 1.0 / p
                scale = jnp.where(row8 == i, lax.rsqrt(p), scale)
                f = jnp.where(row > i, cs[i] * rp, 0.0)
                for m in range(i + 1, 8):
                    cs[m] = cs[m] - f * cs[m][i:i + 1, :]
                x = x - f * x[i:i + 1, :]
                y = y - f * y[i:i + 1, :]
            done_x.append(x[:8] * scale)
            done_y.append(y[:8] * scale)
            x, y = x[8:], y[8:]
        ux = jnp.concatenate(done_x, axis=0)
        uy = jnp.concatenate(done_y, axis=0)
        us.append(ux)
        es.append(uy)
        if h < 3:
            n = 128 - 32 * (h + 1)
            left = ux[:, :]
            d = d[32:] - tdot(left, ux)[32 * (h + 1):]
            e = e[32:] - tdot(left, uy)[32 * (h + 1):]
    return jnp.concatenate(us, axis=0), jnp.concatenate(es, axis=0)


def kernel(data_h, scale_h, ids_h, live_rows_h, live_blocks_h, reg_h, out,
           data, scale, ids, live_rows, live_blocks, reg, own, panel,
           gat, lbuf, rbuf, part, land0, land1, land, res, x_ref,
           ins, w1s, w1f, w1r, w2s, w2r, ps, pr, own_s, own_r, sib_s, sib_r):
    loads = [pltpu.make_async_copy(a, b, ins.at[i]) for i, (a, b) in enumerate((
        (ids_h, ids), (live_rows_h, live_rows), (live_blocks_h, live_blocks), (scale_h, scale),
        (data_h.at[0], data.at[0]), (data_h.at[1], data.at[1]), (data_h.at[2], data.at[2]),
        (data_h.at[3], data.at[3]), (reg_h, reg)))]
    for load in loads:
        load.start()
    r = lax.axis_index("row")
    q = lax.axis_index("col")
    z, yh = r // 2, lax.rem(r, 2)
    zh, zl = z // 2, lax.rem(z, 2)
    yl, j = q // 8, lax.rem(q, 8)
    x, e = j // 2, lax.rem(j, 2)
    xh, xl = x // 2, lax.rem(x, 2)
    pos = 2 * r + yl
    cls = 2 * yl + xh
    kr, kc = 2 * zl + yh, 2 * xl + e
    sibling = (r, q + 1 - 2 * e)
    order = ((0, 3), (1, 2))

    def ring(d):
        x2 = lax.rem(x + d, 4)
        return (r, yl * 8 + 2 * x2 + e), 2 * x2 + e

    def plane(p):
        return (p // 2, lax.rem(p, 2) * 8 + j)

    def remote(src, dst, send, recv, to):
        return pltpu.make_async_remote_copy(src_ref=src, dst_ref=dst, send_sem=send, recv_sem=recv,
                                            device_id=to, device_id_type=MESH)

    barrier = pltpu.get_barrier_semaphore()
    for d in range(1, 4):
        pl.semaphore_signal(barrier, inc=1, device_id=ring(d)[0], device_id_type=MESH)
    pl.semaphore_signal(barrier, inc=1, device_id=sibling, device_id_type=MESH)
    for d in range(1, 16):
        pl.semaphore_signal(barrier, inc=1, device_id=plane(lax.rem(pos + d, 16)), device_id_type=MESH)

    def prepare(s):
        row = lax.broadcasted_iota(jnp.int32, (16, 128), 0)
        on = s < live_blocks[0]
        meta = jnp.where(row == 0, jnp.broadcast_to(scale[...].astype(jnp.float32)[s:s + 1, :], (16, 128)), 0.0)
        for k in range(4):
            keep = jnp.where(on & (k < live_rows[s]), 1.0, 0.0)
            gat[s, j, k * 128:k * 128 + 128, :] = (data[s, k].astype(jnp.float32) * keep).astype(jnp.bfloat16)
            late = jnp.where(ids[s, k] >= 16, 1.0, 0.0)
            meta = jnp.where(row == k + 1, late, meta)
        gat[s, j, 512:528, :] = meta.astype(jnp.bfloat16)

    def send_w1(s):
        for d in (1, 3, 2, 0):
            remote(gat.at[s, j], gat.at[s, j], w1s.at[s], w1r.at[s, j], sibling if d == 0 else ring(d)[0]).start()

    def w1_arrived(s, j2):
        remote(gat.at[s, j2], gat.at[s, j2], w1f.at[s], w1r.at[s, j2], sibling).wait_recv()

    def forward(s):
        for d in (1, 3, 2):
            j2 = ring(d)[1]
            w1_arrived(s, j2)
            remote(gat.at[s, j2], gat.at[s, j2], w1f.at[s], w1r.at[s, j2], sibling).start()

    def compute(s):
        w1_arrived(s, 2 * x + 1 - e)
        for d in (1, 3, 2):
            w1_arrived(s, 2 * lax.rem(x + d, 4) + 1 - e)

        def build(c, _):
            meta = gat[s, c, 512:528, :].astype(jnp.float32)
            sc = meta[0:1, :]
            at = pl.multiple_of(c * 128, 128)
            for k in range(2):
                t = jnp.where(xh == 0, meta[1 + k:2 + k, :], meta[3 + k:4 + k, :])
                a = gat[s, c, pl.ds(pl.multiple_of((2 * xh + k) * 128, 128), 128), :].astype(jnp.float32)
                g = (a * sc).astype(jnp.bfloat16).astype(jnp.float32)
                lbuf[2 * k * 128:2 * k * 128 + 128, pl.ds(at, 128)] = (g * (1.0 - t)).astype(jnp.bfloat16)
                lbuf[2 * k * 128 + 128:2 * k * 128 + 256, pl.ds(at, 128)] = (g * t).astype(jnp.bfloat16)
            t0 = jnp.where(e == 0, meta[1:2, :], meta[2:3, :])
            t1 = jnp.where(e == 0, meta[3:4, :], meta[4:5, :])
            t = jnp.where(xl == 0, t0, t1)
            a = gat[s, c, pl.ds(pl.multiple_of(kc * 128, 128), 128), :].astype(jnp.float32)
            rbuf[0:128, pl.ds(at, 128)] = (a * (1.0 - t)).astype(jnp.bfloat16)
            rbuf[128:256, pl.ds(at, 128)] = (a * t).astype(jnp.bfloat16)
            return 0

        lax.fori_loop(0, 8, build, 0)
        for k in range(2):
            for t in range(2):
                row = (2 * k + t) * 128
                acc = lax.dot_general(lbuf[row:row + 128, :], rbuf[...], (((1,), (1,)), ((), ())),
                                      preferred_element_type=jnp.float32)
                for u in range(2):
                    part[s, :, order[t][u], k] = acc[:, u * 128:u * 128 + 128].reshape(16, 8, 128)

    def w2(s, d, first, count, to_buf, sem):
        to = lax.rem(pos + d, 16)
        return remote(part.at[s, to, first:first + count], to_buf.at[pos], w2s.at[sem], w2r.at[sem], plane(to))

    def w2_wait(buf, sem):
        remote(buf.at[0:15], buf.at[0:15], w2s.at[sem], w2r.at[sem], sibling).wait_recv()

    def w2_sum(mine, buf):
        total = mine
        for d in range(1, 16):
            total = total + buf[lax.rem(pos + d, 16)]
        return total

    def owner_of(s, k):
        sh, sl = s // 2, lax.rem(s, 2)
        to = ((2 * sl + xh) * 2 + k, sh * 8 + (2 * sl + xl) * 2 + e)
        return to, (to[0] != r) | (to[1] != q)

    def to_panel(t):
        for d in range(8):
            to = ((d // 4) * 2 + (d // 2) % 2, (d % 2) * 2 + 1 - e)
            remote(res.at[0, t], panel.at[e, t, xl, xh, pos], ps.at[t], pr.at[t], to).start()

    def panel_sent(t):
        remote(land0.at[0:8], land0.at[0:8], ps.at[t], pr.at[t], sibling).wait_send()

    def leading():
        for d in range(1, 16):
            w2(0, d, 0, 1, land0, 0).start()
        w2_wait(land0, 0)
        res[0, 0:1] = w2_sum(part[0, pos, 0:1], land0)
        to_panel(0)

    def below_start():
        panel_sent(0)
        for d in range(1, 16):
            w2(0, d, 1, 2, land1, 1).start()

    def below():
        w2_wait(land1, 1)
        res[0, 1:3] = w2_sum(part[0, pos, 1:3], land1)
        to_panel(1)
        for k in range(2):
            to, away = owner_of(0, k)
            pl.when(away)(remote(res.at[0, 2, k], own.at[pos, 2], own_s.at[0, k], own_r, to).start)

            @pl.when(jnp.logical_not(away))
            def _():
                own[pos, 2] = res[0, 2, k]

    def send_w2(s):
        for d in range(1, 16):
            w2(s, d, 0, 4, land.at[s - 1], s + 1).start()

    def others(s, _):
        w2_wait(land.at[s - 1], s + 1)
        res[s] = w2_sum(part[s, pos], land.at[s - 1])
        for k in range(2):
            to, away = owner_of(s, k)
            pl.when(away)(remote(res.at[s, :, k], own.at[pos], own_s.at[s, k], own_r, to).start)

            @pl.when(jnp.logical_not(away))
            def _():
                own[pos] = res[s, :, k]
        return 0

    def sent():
        def one(s, _):
            remote(gat.at[s, 0:4], gat.at[s, 0:4], w1s.at[s], w1r.at[s, 0], sibling).wait_send()
            remote(gat.at[s, 0:3], gat.at[s, 0:3], w1f.at[s], w1r.at[s, 0], sibling).wait_send()
            return 0

        lax.fori_loop(0, 4, one, 0)
        for buf, sem in ((land0, 0), (land1, 1), (land.at[0], 2), (land.at[1], 3), (land.at[2], 4)):
            remote(buf.at[0:15], buf.at[0:15], w2s.at[sem], w2r.at[sem], sibling).wait_send()
        def pieces(s, _):
            for k in range(2):
                to, away = owner_of(s, k)
                pl.when(away)(remote(res.at[s, :, k], own.at[pos], own_s.at[s, k], own_r, to).wait_send)
            return 0

        for k in range(2):
            to, away = owner_of(0, k)
            pl.when(away)(remote(res.at[0, 2, k], own.at[pos, 2], own_s.at[0, k], own_r, to).wait_send)
        lax.fori_loop(1, 4, pieces, 0)

    eye = (lax.broadcasted_iota(jnp.int32, (128, 128), 0) == lax.broadcasted_iota(jnp.int32, (128, 128), 1))

    def diag(block):
        return jnp.where(eye, jnp.broadcast_to(reg[pl.ds(block, 1), :], (128, 128)), 0.0)

    def blk(t, a, b):
        return panel[b % 2 if isinstance(b, int) else lax.rem(b, 2), t, b // 2, a // 2, :,
                     a % 2 if isinstance(a, int) else lax.rem(a, 2)].reshape(128, 128)

    def mine(t, u):
        base = own[:, order[t][u]].reshape(128, 128)
        if t == u:
            base = base + jnp.where(kr == kc, 1.0, 0.0) * diag(cls * 4 + kr + 16 * t)
        return base

    def panel_half(t):
        remote(panel.at[1 - e, t], panel.at[1 - e, t], ps.at[t], pr.at[t], sibling).wait_recv()
        remote(panel.at[1 - e, t], panel.at[1 - e, t], sib_s.at[t], sib_r.at[t], sibling).start()

    def panel_rest(t):
        copy = remote(panel.at[1 - e, t], panel.at[e, t], sib_s.at[t], sib_r.at[t], sibling)
        copy.wait_recv()
        copy.wait_send()

    def own_wait(view):
        alone = xh == zl

        @pl.when(alone)
        def _():
            ref = view(15)
            remote(ref, ref, own_s.at[0, 0], own_r, sibling).wait_recv()

        @pl.when(jnp.logical_not(alone))
        def _():
            ref = view(16)
            remote(ref, ref, own_s.at[0, 0], own_r, sibling).wait_recv()

    def factor():
        panel_half(0)
        forward(1)
        below()
        panel_rest(0)
        for i in range(4):
            for k in range(i, 4):
                s = 0.5 * (blk(0, i, k) + blk(0, k, i).T)
                if i == k:
                    s = s + diag(i)
                x_ref[i * 128:i * 128 + 128, k * 128:k * 128 + 128] = s
            x_ref[i * 128:i * 128 + 128, 512:640] = blk(0, kr, i).T + jnp.where(kr == i, 1.0, 0.0) * diag(i)
        inverses = []
        for n in range(4):
            lo, hi = n * 128, n * 128 + 128
            width = 640 if n < 2 else NA
            ud, li = diag_factor(x_ref[lo:hi, lo:hi])
            inverses.append(li)
            if n == 2:
                panel_rest(1)
                for k in range(4):
                    x_ref[k * 128:k * 128 + 128, 640:768] = blk(1, kr, k).T
                    x_ref[k * 128:k * 128 + 128, 768:896] = blk(1, kc, k).T
                for k in range(2):
                    rows, later = slice(k * 128, k * 128 + 128), slice(k * 128 + 128, 512)
                    u = fdot(inverses[k], x_ref[rows, 640:NA])
                    x_ref[rows, 640:NA] = u
                    x_ref[later, 640:NA] = x_ref[later, 640:NA] - tdot(x_ref[rows, later], u)
            u = fdot(li, x_ref[lo:hi, hi:width])
            x_ref[lo:hi, hi:width] = u
            for nxt in range(n + 1, 4):
                c = nxt * 128
                x_ref[c:c + 128, c:width] = x_ref[c:c + 128, c:width] - tdot(u[:, c - hi:c - hi + 128], u[:, c - hi:])
            if n == 0:
                panel_sent(1)
                compute(1)
                send_w2(1)
                forward(2)
                compute(2)
                send_w2(2)
                forward(3)
            if n == 1:
                panel_half(1)
                compute(3)
                send_w2(3)
            if n == 2:
                others(1, 0)
                others(2, 0)
            if n == 3:
                others(3, 0)
        at = pl.multiple_of(kc * 128, 128)
        out[0:128, 0:128] = x_ref[pl.ds(at, 128), 512:640].T
        out[256:384, 0:128] = x_ref[pl.ds(at, 128), 640:768].T
        left = tdot(x_ref[:, 640:768], x_ref[:, 768:896])
        own_wait(lambda n: own.at[0:n, 2])
        out[256:384, 128:256] = mine(1, 1) - left

    for i in range(5):
        loads[i].wait()
    prepare(0)
    pl.semaphore_wait(barrier, 19)
    send_w1(0)
    for s in range(1, 4):
        loads[s + 4].wait()
        prepare(s)
    loads[8].wait()
    out[...] = jnp.zeros_like(out)
    forward(0)
    send_w1(1)
    compute(0)
    leading()
    below_start()
    send_w1(2)
    send_w1(3)

    first_owner = (cls == 0) & (zh == 0)
    pl.when(first_owner)(factor)

    @pl.when(jnp.logical_not(first_owner))
    def _():
        forward(1)
        compute(1)
        below()
        panel_sent(1)
        send_w2(1)
        forward(2)
        compute(2)
        send_w2(2)
        forward(3)
        compute(3)
        send_w2(3)
        lax.fori_loop(1, 4, others, 0)

    @pl.when((cls > 0) & (zh == xh))
    def _():
        own_wait(lambda n: own.at[0:n])
        for t in range(2):
            at = pl.multiple_of((cls // 2 + 2 * t) * 128, 128)
            for u in range(2):
                out[pl.ds(at, 128), u * 128:u * 128 + 128] = mine(t, u)

    sent()


def body(col_data, col_scale, row_ids, live_rows, live_blocks, row_reg):
    anywhere = pl.BlockSpec(memory_space=pl.ANY)
    dma = pltpu.SemaphoreType.DMA
    return pl.pallas_call(
        kernel,
        out_shape=jax.ShapeDtypeStruct((512, 256), jnp.float32),
        in_specs=[anywhere] * 6,
        out_specs=pl.BlockSpec(memory_space=pltpu.VMEM),
        scratch_shapes=[
            pltpu.VMEM((4, 4, 128, 128), jnp.bfloat16),
            pltpu.VMEM((4, 128), jnp.bfloat16),
            pltpu.SMEM((4, 4), jnp.int32),
            pltpu.SMEM((4,), jnp.int32),
            pltpu.SMEM((1,), jnp.int32),
            pltpu.VMEM((32, 128), jnp.float32),
            pltpu.VMEM((16, 4, 8, 128), jnp.float32),
            pltpu.VMEM((2, 2, 2, 2, 16, 2, 8, 128), jnp.float32),
            pltpu.VMEM((4, 8, ROWS, 128), jnp.bfloat16),
            pltpu.VMEM((512, 1024), jnp.bfloat16),
            pltpu.VMEM((256, 1024), jnp.bfloat16),
            pltpu.VMEM((4, 16, 4, 2, 8, 128), jnp.float32),
            pltpu.VMEM((16, 1, 2, 8, 128), jnp.float32),
            pltpu.VMEM((16, 2, 2, 8, 128), jnp.float32),
            pltpu.VMEM((3, 16, 4, 2, 8, 128), jnp.float32),
            pltpu.VMEM((4, 4, 2, 8, 128), jnp.float32),
            pltpu.VMEM((512, NA), jnp.float32),
            dma((9,)),
            dma((4,)), dma((4,)), dma((4, 8)), dma((5,)), dma((5,)), dma((2,)), dma((2,)),
            dma((4, 2)), dma, dma((2,)), dma((2,)),
        ],
        compiler_params=pltpu.CompilerParams(
            collective_id=0, has_side_effects=True, vmem_limit_bytes=60 * 1024 * 1024),
    )(col_data, col_scale, row_ids, live_rows, live_blocks, row_reg.reshape(32, 128))


def solution(mesh):
    return jax.shard_map(
        body,
        mesh=mesh,
        in_specs=(
            P(("row", "col"), None, None, None),
            P(("row", "col"), None),
            P(("row", "col"), None),
            P(("row", "col")),
            P(("row", "col")),
            P(),
        ),
        out_specs=P("row", "col"),
        check_vma=False,
    )
```

```python
import jax
import jax.numpy as jnp
from jax import lax
from jax.experimental import pallas as pl
from jax.experimental.pallas import tpu as pltpu
from jax.sharding import PartitionSpec as P

HI = lax.Precision.HIGHEST
NA = 896
ROWS = 528
MESH = pl.DeviceIdType.MESH


def tdot(a, b):
    return lax.dot_general(a, b, (((0,), (0,)), ((), ())), precision=HI,
                           preferred_element_type=jnp.float32)


def fdot(a, b):
    return jnp.dot(a, b, precision=HI, preferred_element_type=jnp.float32)


def lanes(v):
    return jnp.broadcast_to(v, (v.shape[0], 128))


def diag_factor(d, between=None):
    row8 = lax.broadcasted_iota(jnp.int32, (8, 128), 0)
    e = jnp.where(lax.broadcasted_iota(jnp.int32, (128, 128), 0) == lax.broadcasted_iota(jnp.int32, (128, 128), 1), 1.0, 0.0)
    us, es = [], []
    for h in range(4):
        x, y = d[:32], e[:32]
        done_x, done_y = [], []
        for j in range(4):
            lane = 32 * h + 8 * j
            rows = 32 - 8 * j
            row = lax.broadcasted_iota(jnp.int32, (rows, 128), 0)
            cs = [lanes(x[:, lane + i:lane + i + 1]) for i in range(8)]
            scale = jnp.zeros((8, 128), jnp.float32)
            for i in range(8):
                p = cs[i][i:i + 1, :]
                rp = 1.0 / p
                scale = jnp.where(row8 == i, lax.rsqrt(p), scale)
                f = jnp.where(row > i, cs[i] * rp, 0.0)
                for m in range(i + 1, 8):
                    cs[m] = cs[m] - f * cs[m][i:i + 1, :]
                x = x - f * x[i:i + 1, :]
                y = y - f * y[i:i + 1, :]
            done_x.append(x[:8] * scale)
            done_y.append(y[:8] * scale)
            x, y = x[8:], y[8:]
        ux = jnp.concatenate(done_x, axis=0)
        uy = jnp.concatenate(done_y, axis=0)
        us.append(ux)
        es.append(uy)
        if h < 3:
            n = 128 - 32 * (h + 1)
            left = ux[:, :]
            d = d[32:] - tdot(left, ux)[32 * (h + 1):]
            e = e[32:] - tdot(left, uy)[32 * (h + 1):]
    return jnp.concatenate(us, axis=0), jnp.concatenate(es, axis=0)


def kernel(data_h, scale_h, ids_h, live_rows_h, live_blocks_h, reg_h, out,
           data, scale, ids, live_rows, live_blocks, reg, own, panel,
           gat, lbuf, rbuf, part, land0, land1, land, res, x_ref,
           ins, w1s, w1f, w1r, w2s, w2r, ps, pr, own_s, own_r, sib_s, sib_r):
    loads = [pltpu.make_async_copy(a, b, ins.at[i]) for i, (a, b) in enumerate((
        (ids_h, ids), (live_rows_h, live_rows), (live_blocks_h, live_blocks), (scale_h, scale),
        (data_h.at[0], data.at[0]), (data_h.at[1], data.at[1]), (data_h.at[2], data.at[2]),
        (data_h.at[3], data.at[3]), (reg_h, reg)))]
    for load in loads:
        load.start()
    r = lax.axis_index("row")
    q = lax.axis_index("col")
    z, yh = r // 2, lax.rem(r, 2)
    zh, zl = z // 2, lax.rem(z, 2)
    yl = q // 8
    x, e = lax.rem(q, 8) // 2, lax.rem(q, 2)
    xh, xl = x // 2, lax.rem(x, 2)
    y = 2 * yh + yl
    cls = 2 * yl + xh
    kr, kc = 2 * zl + yh, 2 * xl + e
    sibling = (r, q + 1 - 2 * e)
    order = ((0, 3), (1, 2))
    along = (x, y, z, z)
    place = (4 * z + y, 4 * z + x, 4 * y + x, 4 * y + x)

    def device(xx, yy, zz):
        return (2 * zz + yy // 2, lax.rem(yy, 2) * 8 + 2 * xx + e)

    def ring(s, d):
        u = lax.rem(along[s] + d, 4)
        to = (device(u, y, z), device(x, u, z), device(x, y, u), device(x, y, u))[s]
        return to, 2 * u + e

    def plane(s, p):
        a, b = p // 4, lax.rem(p, 4)
        return (device(x, b, a), device(b, y, a), device(b, a, z), device(b, a, z))[s]

    def remote(src, dst, send, recv, to):
        return pltpu.make_async_remote_copy(src_ref=src, dst_ref=dst, send_sem=send, recv_sem=recv,
                                            device_id=to, device_id_type=MESH)

    barrier = pltpu.get_barrier_semaphore()
    pl.semaphore_signal(barrier, inc=1, device_id=sibling, device_id_type=MESH)
    for dx in range(4):
        for dy in range(4):
            for dz in range(4):
                if 0 < (dx > 0) + (dy > 0) + (dz > 0) < 3:
                    to = device(lax.rem(x + dx, 4), lax.rem(y + dy, 4), lax.rem(z + dz, 4))
                    pl.semaphore_signal(barrier, inc=1, device_id=to, device_id_type=MESH)

    def prepare(s):
        j = 2 * along[s] + e
        row = lax.broadcasted_iota(jnp.int32, (16, 128), 0)
        on = s < live_blocks[0]
        meta = jnp.where(row == 0, jnp.broadcast_to(scale[...].astype(jnp.float32)[s:s + 1, :], (16, 128)), 0.0)
        for k in range(4):
            keep = jnp.where(on & (k < live_rows[s]), 1.0, 0.0)
            gat[s, j, k * 128:k * 128 + 128, :] = (data[s, k].astype(jnp.float32) * keep).astype(jnp.bfloat16)
            late = jnp.where(ids[s, k] >= 16, 1.0, 0.0)
            meta = jnp.where(row == k + 1, late, meta)
        gat[s, j, 512:528, :] = meta.astype(jnp.bfloat16)

    def send_w1(s):
        j = 2 * along[s] + e
        for d in (1, 3, 2, 0):
            remote(gat.at[s, j], gat.at[s, j], w1s.at[s], w1r.at[s, j], sibling if d == 0 else ring(s, d)[0]).start()

    def w1_arrived(s, j2):
        remote(gat.at[s, j2], gat.at[s, j2], w1f.at[s], w1r.at[s, j2], sibling).wait_recv()

    def forward(s):
        for d in (1, 3, 2):
            j2 = ring(s, d)[1]
            w1_arrived(s, j2)
            remote(gat.at[s, j2], gat.at[s, j2], w1f.at[s], w1r.at[s, j2], sibling).start()

    def compute(s):
        u = along[s]
        uh, ul = u // 2, lax.rem(u, 2)
        for d in (0, 1, 3, 2):
            w1_arrived(s, 2 * lax.rem(u + d, 4) + 1 - e)

        def build(c, _):
            meta = gat[s, c, 512:528, :].astype(jnp.float32)
            sc = meta[0:1, :]
            at = pl.multiple_of(c * 128, 128)
            for k in range(2):
                t = jnp.where(uh == 0, meta[1 + k:2 + k, :], meta[3 + k:4 + k, :])
                a = gat[s, c, pl.ds(pl.multiple_of((2 * uh + k) * 128, 128), 128), :].astype(jnp.float32)
                g = (a * sc).astype(jnp.bfloat16).astype(jnp.float32)
                lbuf[2 * k * 128:2 * k * 128 + 128, pl.ds(at, 128)] = (g * (1.0 - t)).astype(jnp.bfloat16)
                lbuf[2 * k * 128 + 128:2 * k * 128 + 256, pl.ds(at, 128)] = (g * t).astype(jnp.bfloat16)
            t0 = jnp.where(e == 0, meta[1:2, :], meta[2:3, :])
            t1 = jnp.where(e == 0, meta[3:4, :], meta[4:5, :])
            t = jnp.where(ul == 0, t0, t1)
            a = gat[s, c, pl.ds(pl.multiple_of((2 * ul + e) * 128, 128), 128), :].astype(jnp.float32)
            rbuf[0:128, pl.ds(at, 128)] = (a * (1.0 - t)).astype(jnp.bfloat16)
            rbuf[128:256, pl.ds(at, 128)] = (a * t).astype(jnp.bfloat16)
            return 0

        lax.fori_loop(0, 8, build, 0)
        for k in range(2):
            for t in range(2):
                row = (2 * k + t) * 128
                acc = lax.dot_general(lbuf[row:row + 128, :], rbuf[...], (((1,), (1,)), ((), ())),
                                      preferred_element_type=jnp.float32)
                for u in range(2):
                    part[s, :, order[t][u], k] = acc[:, u * 128:u * 128 + 128].reshape(16, 8, 128)

    def w2(s, d, first, count, to_buf, sem):
        to = lax.rem(place[s] + d, 16)
        return remote(part.at[s, to, first:first + count], to_buf.at[place[s]], w2s.at[sem], w2r.at[sem], plane(s, to))

    def w2_wait(buf, sem):
        remote(buf.at[0:15], buf.at[0:15], w2s.at[sem], w2r.at[sem], sibling).wait_recv()

    def w2_sum(s, mine, buf):
        total = mine
        for d in range(1, 16):
            total = total + buf[lax.rem(place[s] + d, 16)]
        return total

    def owner_of(s, k):
        uh, ul = along[s] // 2, lax.rem(along[s], 2)
        to = device(2 * (s % 2) + ul, 2 * k + s // 2, 2 * (s % 2) + uh)
        return to, (to[0] != r) | (to[1] != q)

    def to_panel(t):
        for d in range(8):
            to = ((d // 4) * 2 + (d // 2) % 2, (d % 2) * 2 + 1 - e)
            remote(res.at[0, t], panel.at[e, t, xl, xh, place[0]], ps.at[t], pr.at[t], to).start()

    def panel_sent(t):
        remote(land0.at[0:8], land0.at[0:8], ps.at[t], pr.at[t], sibling).wait_send()

    def leading_start():
        for d in range(1, 16):
            w2(0, d, 0, 1, land0, 0).start()

    def leading():
        w2_wait(land0, 0)
        res[0, 0:1] = w2_sum(0, part[0, place[0], 0:1], land0)
        to_panel(0)

    def below_start():
        for d in range(1, 16):
            w2(0, d, 1, 2, land1, 1).start()

    def below():
        w2_wait(land1, 1)
        res[0, 1:3] = w2_sum(0, part[0, place[0], 1:3], land1)
        to_panel(1)
        for k in range(2):
            to, away = owner_of(0, k)
            pl.when(away)(remote(res.at[0, 2, k], own.at[place[0], 2], own_s.at[0, k], own_r, to).start)

            @pl.when(jnp.logical_not(away))
            def _():
                own[place[0], 2] = res[0, 2, k]

    def send_w2(s):
        for d in range(1, 16):
            w2(s, d, 0, 4, land.at[s - 1], s + 1).start()

    def others(s):
        w2_wait(land.at[s - 1], s + 1)
        res[s] = w2_sum(s, part[s, place[s]], land.at[s - 1])
        for k in range(2):
            to, away = owner_of(s, k)
            pl.when(away)(remote(res.at[s, :, k], own.at[place[s]], own_s.at[s, k], own_r, to).start)

            @pl.when(jnp.logical_not(away))
            def _():
                own[place[s]] = res[s, :, k]

    def sent():
        def one(s, _):
            remote(gat.at[s, 0:4], gat.at[s, 0:4], w1s.at[s], w1r.at[s, 0], sibling).wait_send()
            remote(gat.at[s, 0:3], gat.at[s, 0:3], w1f.at[s], w1r.at[s, 0], sibling).wait_send()
            return 0

        lax.fori_loop(0, 4, one, 0)
        for buf, sem in ((land0, 0), (land1, 1), (land.at[0], 2), (land.at[1], 3), (land.at[2], 4)):
            remote(buf.at[0:15], buf.at[0:15], w2s.at[sem], w2r.at[sem], sibling).wait_send()
        for k in range(2):
            to, away = owner_of(0, k)
            pl.when(away)(remote(res.at[0, 2, k], own.at[place[0], 2], own_s.at[0, k], own_r, to).wait_send)
        for s in range(1, 4):
            for k in range(2):
                to, away = owner_of(s, k)
                pl.when(away)(remote(res.at[s, :, k], own.at[place[s]], own_s.at[s, k], own_r, to).wait_send)

    eye = (lax.broadcasted_iota(jnp.int32, (128, 128), 0) == lax.broadcasted_iota(jnp.int32, (128, 128), 1))

    def diag(block):
        return jnp.where(eye, jnp.broadcast_to(reg[pl.ds(block, 1), :], (128, 128)), 0.0)

    def blk(t, a, b):
        return panel[b % 2 if isinstance(b, int) else lax.rem(b, 2), t, b // 2, a // 2, :,
                     a % 2 if isinstance(a, int) else lax.rem(a, 2)].reshape(128, 128)

    def mine(t, u):
        base = own[:, order[t][u]].reshape(128, 128)
        if t == u:
            base = base + jnp.where(kr == kc, 1.0, 0.0) * diag(cls * 4 + kr + 16 * t)
        return base

    def panel_half(t):
        remote(panel.at[1 - e, t], panel.at[1 - e, t], ps.at[t], pr.at[t], sibling).wait_recv()
        remote(panel.at[1 - e, t], panel.at[1 - e, t], sib_s.at[t], sib_r.at[t], sibling).start()

    def panel_rest(t):
        copy = remote(panel.at[1 - e, t], panel.at[e, t], sib_s.at[t], sib_r.at[t], sibling)
        copy.wait_recv()
        copy.wait_send()

    def own_wait(view):
        mark = 2 * zl + xl
        alone = ((cls == 0) & (x == mark)) | ((cls == 1) & (y == mark)) | ((cls > 1) & (z == mark))

        @pl.when(alone)
        def _():
            ref = view(15)
            remote(ref, ref, own_s.at[0, 0], own_r, sibling).wait_recv()

        @pl.when(jnp.logical_not(alone))
        def _():
            ref = view(16)
            remote(ref, ref, own_s.at[0, 0], own_r, sibling).wait_recv()

    def factor():
        panel_half(0)
        compute(1)
        below()
        panel_rest(0)
        for i in range(4):
            for k in range(i, 4):
                s = 0.5 * (blk(0, i, k) + blk(0, k, i).T)
                if i == k:
                    s = s + diag(i)
                x_ref[i * 128:i * 128 + 128, k * 128:k * 128 + 128] = s
            x_ref[i * 128:i * 128 + 128, 512:640] = blk(0, kr, i).T + jnp.where(kr == i, 1.0, 0.0) * diag(i)
        inverses = []
        for n in range(4):
            lo, hi = n * 128, n * 128 + 128
            width = 640 if n < 2 else NA
            ud, li = diag_factor(x_ref[lo:hi, lo:hi])
            inverses.append(li)
            if n == 2:
                panel_rest(1)
                for k in range(4):
                    x_ref[k * 128:k * 128 + 128, 640:768] = blk(1, kr, k).T
                    x_ref[k * 128:k * 128 + 128, 768:896] = blk(1, kc, k).T
                for k in range(2):
                    rows, later = slice(k * 128, k * 128 + 128), slice(k * 128 + 128, 512)
                    u = fdot(inverses[k], x_ref[rows, 640:NA])
                    x_ref[rows, 640:NA] = u
                    x_ref[later, 640:NA] = x_ref[later, 640:NA] - tdot(x_ref[rows, later], u)
            u = fdot(li, x_ref[lo:hi, hi:width])
            x_ref[lo:hi, hi:width] = u
            for nxt in range(n + 1, 4):
                c = nxt * 128
                x_ref[c:c + 128, c:width] = x_ref[c:c + 128, c:width] - tdot(u[:, c - hi:c - hi + 128], u[:, c - hi:])
            if n == 0:
                panel_sent(1)
                send_w2(1)
                compute(3)
                send_w2(3)
            if n == 1:
                panel_half(1)
                others(2)
            if n == 2:
                others(1)
                others(3)
            if n == 3:
                pass
        at = pl.multiple_of(kc * 128, 128)
        out[0:128, 0:128] = x_ref[pl.ds(at, 128), 512:640].T
        out[256:384, 0:128] = x_ref[pl.ds(at, 128), 640:768].T
        left = tdot(x_ref[:, 640:768], x_ref[:, 768:896])
        own_wait(lambda n: own.at[0:n, 2])
        out[256:384, 128:256] = mine(1, 1) - left

    for i in range(5):
        loads[i].wait()
    prepare(0)
    pl.semaphore_wait(barrier, 37)
    send_w1(0)
    for s in range(1, 4):
        loads[s + 4].wait()
        prepare(s)
        if s in (1, 2):
            send_w1(s)
    loads[8].wait()
    out[...] = jnp.zeros_like(out)
    forward(0)
    send_w1(3)
    compute(0)
    leading_start()
    leading()
    forward(1)
    forward(2)
    panel_sent(0)
    below_start()
    compute(2)
    send_w2(2)
    forward(3)

    first_owner = (cls == 0) & (zh == 0)
    pl.when(first_owner)(factor)

    @pl.when(jnp.logical_not(first_owner))
    def _():
        compute(1)
        below()
        panel_sent(1)
        send_w2(1)
        compute(3)
        send_w2(3)
        others(2)
        others(1)
        others(3)

    @pl.when((cls > 0) & (zh == xh))
    def _():
        own_wait(lambda n: own.at[0:n])
        for t in range(2):
            at = pl.multiple_of((cls // 2 + 2 * t) * 128, 128)
            for u in range(2):
                out[pl.ds(at, 128), u * 128:u * 128 + 128] = mine(t, u)

    sent()


def body(col_data, col_scale, row_ids, live_rows, live_blocks, row_reg):
    anywhere = pl.BlockSpec(memory_space=pltpu.HBM)
    dma = pltpu.SemaphoreType.DMA
    return pl.pallas_call(
        kernel,
        out_shape=jax.ShapeDtypeStruct((512, 256), jnp.float32),
        in_specs=[anywhere] * 6,
        out_specs=pl.BlockSpec(memory_space=pltpu.VMEM),
        scratch_shapes=[
            pltpu.VMEM((4, 4, 128, 128), jnp.bfloat16),
            pltpu.VMEM((4, 128), jnp.bfloat16),
            pltpu.SMEM((4, 4), jnp.int32),
            pltpu.SMEM((4,), jnp.int32),
            pltpu.SMEM((1,), jnp.int32),
            pltpu.VMEM((32, 128), jnp.float32),
            pltpu.VMEM((16, 4, 8, 128), jnp.float32),
            pltpu.VMEM((2, 2, 2, 2, 16, 2, 8, 128), jnp.float32),
            pltpu.VMEM((4, 8, ROWS, 128), jnp.bfloat16),
            pltpu.VMEM((512, 1024), jnp.bfloat16),
            pltpu.VMEM((256, 1024), jnp.bfloat16),
            pltpu.VMEM((4, 16, 4, 2, 8, 128), jnp.float32),
            pltpu.VMEM((16, 1, 2, 8, 128), jnp.float32),
            pltpu.VMEM((16, 2, 2, 8, 128), jnp.float32),
            pltpu.VMEM((3, 16, 4, 2, 8, 128), jnp.float32),
            pltpu.VMEM((4, 4, 2, 8, 128), jnp.float32),
            pltpu.VMEM((512, NA), jnp.float32),
            dma((9,)),
            dma((4,)), dma((4,)), dma((4, 8)), dma((5,)), dma((5,)), dma((2,)), dma((2,)),
            dma((4, 2)), dma, dma((2,)), dma((2,)),
        ],
        compiler_params=pltpu.CompilerParams(
            collective_id=0, has_side_effects=True, vmem_limit_bytes=60 * 1024 * 1024),
    )(col_data, col_scale, row_ids, live_rows, live_blocks, row_reg.reshape(32, 128))


def solution(mesh):
    return jax.shard_map(
        body,
        mesh=mesh,
        in_specs=(
            P(("row", "col"), None, None, None),
            P(("row", "col"), None),
            P(("row", "col"), None),
            P(("row", "col")),
            P(("row", "col")),
            P(),
        ),
        out_specs=P("row", "col"),
        check_vma=False,
    )
```

```python
import jax
import jax.numpy as jnp
from jax import lax
from jax.experimental import pallas as pl
from jax.experimental.pallas import tpu as pltpu
from jax.sharding import PartitionSpec as P

HI = lax.Precision.HIGHEST
NA = 896
ROWS = 528
MESH = pl.DeviceIdType.MESH


def tdot(a, b):
    return lax.dot_general(a, b, (((0,), (0,)), ((), ())), precision=HI,
                           preferred_element_type=jnp.float32)


def fdot(a, b):
    return jnp.dot(a, b, precision=HI, preferred_element_type=jnp.float32)


def lanes(v):
    return jnp.broadcast_to(v, (v.shape[0], 128))


def diag_factor(d):
    row8 = lax.broadcasted_iota(jnp.int32, (8, 128), 0)
    e = jnp.where(lax.broadcasted_iota(jnp.int32, (128, 128), 0) == lax.broadcasted_iota(jnp.int32, (128, 128), 1), 1.0, 0.0)
    us, es = [], []
    for h in range(4):
        x, y = d[:32], e[:32]
        done_x, done_y = [], []
        for j in range(4):
            lane = 32 * h + 8 * j
            rows = 32 - 8 * j
            row = lax.broadcasted_iota(jnp.int32, (rows, 128), 0)
            cs = [lanes(x[:, lane + i:lane + i + 1]) for i in range(8)]
            scale = jnp.zeros((8, 128), jnp.float32)
            for i in range(0, 8, 2):
                a, b, c = cs[i][i:i + 1, :], cs[i + 1][i:i + 1, :], cs[i + 1][i + 1:i + 2, :]
                det = a * c - b * b
                ra, rdet = 1.0 / a, 1.0 / det
                w = b * ra
                scale = jnp.where(row8 == i, lax.rsqrt(a), scale)
                scale = jnp.where(row8 == i + 1, lax.rsqrt(det * ra), scale)
                f = jnp.where(row > i, cs[i] * ra, 0.0)
                g = jnp.where(row > i + 1, (cs[i + 1] - cs[i] * w) * (a * rdet), 0.0)
                for m in range(i + 2, 8):
                    t = cs[m][i:i + 1, :]
                    cs[m] = cs[m] - f * t - g * (cs[m][i + 1:i + 2, :] - w * t)
                t = x[i:i + 1, :]
                x = x - f * t - g * (x[i + 1:i + 2, :] - w * t)
                t = y[i:i + 1, :]
                y = y - f * t - g * (y[i + 1:i + 2, :] - w * t)
            done_x.append(x[:8] * scale)
            done_y.append(y[:8] * scale)
            x, y = x[8:], y[8:]
        ux = jnp.concatenate(done_x, axis=0)
        uy = jnp.concatenate(done_y, axis=0)
        us.append(ux)
        es.append(uy)
        if h < 3:
            d = d[32:] - tdot(ux, ux)[32 * (h + 1):]
            e = e[32:] - tdot(ux, uy)[32 * (h + 1):]
    return jnp.concatenate(us, axis=0), jnp.concatenate(es, axis=0)


def kernel(data_h, scale_h, ids_h, live_rows_h, live_blocks_h, reg_h, out,
           data, scale, ids, live_rows, live_blocks, reg, own, panel,
           gat, lbuf, rbuf, part, land0, land1, land, res, x_ref,
           ins, w1s, w1f, w1r, w2s, w2r, ps, pr, own_s, own_r, sib_s, sib_r):
    loads = [pltpu.make_async_copy(a, b, ins.at[i]) for i, (a, b) in enumerate((
        (ids_h, ids), (live_rows_h, live_rows), (live_blocks_h, live_blocks), (scale_h, scale),
        (data_h.at[0], data.at[0]), (data_h.at[1], data.at[1]), (data_h.at[2], data.at[2]),
        (data_h.at[3], data.at[3]), (reg_h, reg)))]
    for load in loads:
        load.start()
    r = lax.axis_index("row")
    q = lax.axis_index("col")
    z, yh = r // 2, lax.rem(r, 2)
    zh, zl = z // 2, lax.rem(z, 2)
    yl = q // 8
    x, e = lax.rem(q, 8) // 2, lax.rem(q, 2)
    xh, xl = x // 2, lax.rem(x, 2)
    y = 2 * yh + yl
    cls = 2 * yl + xh
    kr, kc = 2 * zl + yh, 2 * xl + e
    sibling = (r, q + 1 - 2 * e)
    order = ((0, 3), (1, 2))
    along = (x, y, z, z)
    place = (4 * z + y, 4 * z + x, 4 * y + x, 4 * y + x)

    def device(xx, yy, zz):
        return (2 * zz + yy // 2, lax.rem(yy, 2) * 8 + 2 * xx + e)

    def ring(s, d):
        u = lax.rem(along[s] + d, 4)
        to = (device(u, y, z), device(x, u, z), device(x, y, u), device(x, y, u))[s]
        return to, 2 * u + e

    def plane(s, p):
        a, b = p // 4, lax.rem(p, 4)
        return (device(x, b, a), device(b, y, a), device(b, a, z), device(b, a, z))[s]

    def remote(src, dst, send, recv, to):
        return pltpu.make_async_remote_copy(src_ref=src, dst_ref=dst, send_sem=send, recv_sem=recv,
                                            device_id=to, device_id_type=MESH)

    barrier = pltpu.get_barrier_semaphore()
    pl.semaphore_signal(barrier, inc=1, device_id=sibling, device_id_type=MESH)
    for dx in range(4):
        for dy in range(4):
            for dz in range(4):
                if 0 < (dx > 0) + (dy > 0) + (dz > 0) < 3:
                    to = device(lax.rem(x + dx, 4), lax.rem(y + dy, 4), lax.rem(z + dz, 4))
                    pl.semaphore_signal(barrier, inc=1, device_id=to, device_id_type=MESH)

    def prepare(s):
        j = 2 * along[s] + e
        row = lax.broadcasted_iota(jnp.int32, (16, 128), 0)
        on = s < live_blocks[0]
        meta = jnp.where(row == 0, jnp.broadcast_to(scale[...].astype(jnp.float32)[s:s + 1, :], (16, 128)), 0.0)
        for k in range(4):
            keep = jnp.where(on & (k < live_rows[s]), 1.0, 0.0)
            gat[s, j, k * 128:k * 128 + 128, :] = (data[s, k].astype(jnp.float32) * keep).astype(jnp.bfloat16)
            late = jnp.where(ids[s, k] >= 16, 1.0, 0.0)
            meta = jnp.where(row == k + 1, late, meta)
        gat[s, j, 512:528, :] = meta.astype(jnp.bfloat16)

    def send_w1(s):
        j = 2 * along[s] + e
        for d in (1, 3, 2, 0):
            remote(gat.at[s, j], gat.at[s, j], w1s.at[s], w1r.at[s, j], sibling if d == 0 else ring(s, d)[0]).start()

    def w1_arrived(s, j2):
        remote(gat.at[s, j2], gat.at[s, j2], w1f.at[s], w1r.at[s, j2], sibling).wait_recv()

    def forward(s):
        for d in (1, 3, 2):
            j2 = ring(s, d)[1]
            w1_arrived(s, j2)
            remote(gat.at[s, j2], gat.at[s, j2], w1f.at[s], w1r.at[s, j2], sibling).start()

    def compute(s):
        u = along[s]
        uh, ul = u // 2, lax.rem(u, 2)
        for d in (0, 1, 3, 2):
            w1_arrived(s, 2 * lax.rem(u + d, 4) + 1 - e)

        def build(c, _):
            meta = gat[s, c, 512:528, :].astype(jnp.float32)
            sc = meta[0:1, :]
            at = pl.multiple_of(c * 128, 128)
            for k in range(2):
                t = jnp.where(uh == 0, meta[1 + k:2 + k, :], meta[3 + k:4 + k, :])
                a = gat[s, c, pl.ds(pl.multiple_of((2 * uh + k) * 128, 128), 128), :].astype(jnp.float32)
                g = (a * sc).astype(jnp.bfloat16).astype(jnp.float32)
                lbuf[2 * k * 128:2 * k * 128 + 128, pl.ds(at, 128)] = (g * (1.0 - t)).astype(jnp.bfloat16)
                lbuf[2 * k * 128 + 128:2 * k * 128 + 256, pl.ds(at, 128)] = (g * t).astype(jnp.bfloat16)
            t0 = jnp.where(e == 0, meta[1:2, :], meta[2:3, :])
            t1 = jnp.where(e == 0, meta[3:4, :], meta[4:5, :])
            t = jnp.where(ul == 0, t0, t1)
            a = gat[s, c, pl.ds(pl.multiple_of((2 * ul + e) * 128, 128), 128), :].astype(jnp.float32)
            rbuf[0:128, pl.ds(at, 128)] = (a * (1.0 - t)).astype(jnp.bfloat16)
            rbuf[128:256, pl.ds(at, 128)] = (a * t).astype(jnp.bfloat16)
            return 0

        lax.fori_loop(0, 8, build, 0)
        multiply(s, 0)
        if s > 0:
            multiply(s, 1)

    def multiply(s, t):
        for k in range(2):
            row = (2 * k + t) * 128
            acc = lax.dot_general(lbuf[row:row + 128, :], rbuf[...], (((1,), (1,)), ((), ())),
                                  preferred_element_type=jnp.float32)
            for u in range(2):
                part[s, :, order[t][u], k] = acc[:, u * 128:u * 128 + 128].reshape(16, 8, 128)

    def w2(s, d, first, count, to_buf, sem):
        to = lax.rem(place[s] + d, 16)
        return remote(part.at[s, to, first:first + count], to_buf.at[place[s]], w2s.at[sem], w2r.at[sem], plane(s, to))

    def w2_wait(buf, sem):
        remote(buf.at[0:15], buf.at[0:15], w2s.at[sem], w2r.at[sem], sibling).wait_recv()

    def w2_sum(s, mine, buf):
        total = mine
        for d in range(1, 16):
            total = total + buf[lax.rem(place[s] + d, 16)]
        return total

    def owner_of(s, k):
        uh, ul = along[s] // 2, lax.rem(along[s], 2)
        to = device(2 * (s % 2) + ul, 2 * k + s // 2, 2 * (s % 2) + uh)
        return to, (to[0] != r) | (to[1] != q)

    def to_panel(t):
        for d in range(8):
            to = ((d // 4) * 2 + (d // 2) % 2, (d % 2) * 2 + 1 - e)
            remote(res.at[0, t], panel.at[e, t, xl, xh, place[0]], ps.at[t], pr.at[t], to).start()

    def panel_sent(t):
        remote(land0.at[0:8], land0.at[0:8], ps.at[t], pr.at[t], sibling).wait_send()

    def leading_start():
        for d in range(1, 16):
            w2(0, d, 0, 1, land0, 0).start()

    def leading():
        w2_wait(land0, 0)
        res[0, 0:1] = w2_sum(0, part[0, place[0], 0:1], land0)
        to_panel(0)

    def below_start():
        for d in range(1, 16):
            w2(0, d, 1, 2, land1, 1).start()

    def below():
        w2_wait(land1, 1)
        res[0, 1:3] = w2_sum(0, part[0, place[0], 1:3], land1)
        to_panel(1)
        for k in range(2):
            to, away = owner_of(0, k)
            pl.when(away)(remote(res.at[0, 2, k], own.at[place[0], 2], own_s.at[0, k], own_r, to).start)

            @pl.when(jnp.logical_not(away))
            def _():
                own[place[0], 2] = res[0, 2, k]

    def send_w2(s):
        for d in range(1, 16):
            w2(s, d, 0, 4, land.at[s - 1], s + 1).start()

    def others(s):
        w2_wait(land.at[s - 1], s + 1)
        res[s] = w2_sum(s, part[s, place[s]], land.at[s - 1])
        for k in range(2):
            to, away = owner_of(s, k)
            pl.when(away)(remote(res.at[s, :, k], own.at[place[s]], own_s.at[s, k], own_r, to).start)

            @pl.when(jnp.logical_not(away))
            def _():
                own[place[s]] = res[s, :, k]

    def sent():
        def one(s, _):
            remote(gat.at[s, 0:4], gat.at[s, 0:4], w1s.at[s], w1r.at[s, 0], sibling).wait_send()
            remote(gat.at[s, 0:3], gat.at[s, 0:3], w1f.at[s], w1r.at[s, 0], sibling).wait_send()
            return 0

        lax.fori_loop(0, 4, one, 0)
        for buf, sem in ((land0, 0), (land1, 1), (land.at[0], 2), (land.at[1], 3), (land.at[2], 4)):
            remote(buf.at[0:15], buf.at[0:15], w2s.at[sem], w2r.at[sem], sibling).wait_send()
        for k in range(2):
            to, away = owner_of(0, k)
            pl.when(away)(remote(res.at[0, 2, k], own.at[place[0], 2], own_s.at[0, k], own_r, to).wait_send)
        for s in range(1, 4):
            for k in range(2):
                to, away = owner_of(s, k)
                pl.when(away)(remote(res.at[s, :, k], own.at[place[s]], own_s.at[s, k], own_r, to).wait_send)

    eye = (lax.broadcasted_iota(jnp.int32, (128, 128), 0) == lax.broadcasted_iota(jnp.int32, (128, 128), 1))

    def diag(block):
        return jnp.where(eye, jnp.broadcast_to(reg[pl.ds(block, 1), :], (128, 128)), 0.0)

    def blk(t, a, b):
        return panel[b % 2 if isinstance(b, int) else lax.rem(b, 2), t, b // 2, a // 2, :,
                     a % 2 if isinstance(a, int) else lax.rem(a, 2)].reshape(128, 128)

    def mine(t, u):
        base = own[:, order[t][u]].reshape(128, 128)
        if t == u:
            base = base + jnp.where(kr == kc, 1.0, 0.0) * diag(cls * 4 + kr + 16 * t)
        return base

    def panel_half(t):
        remote(panel.at[1 - e, t], panel.at[1 - e, t], ps.at[t], pr.at[t], sibling).wait_recv()
        remote(panel.at[1 - e, t], panel.at[1 - e, t], sib_s.at[t], sib_r.at[t], sibling).start()

    def panel_rest(t):
        copy = remote(panel.at[1 - e, t], panel.at[e, t], sib_s.at[t], sib_r.at[t], sibling)
        copy.wait_recv()
        copy.wait_send()

    def own_wait(view):
        mark = 2 * zl + xl
        alone = ((cls == 0) & (x == mark)) | ((cls == 1) & (y == mark)) | ((cls > 1) & (z == mark))

        @pl.when(alone)
        def _():
            ref = view(15)
            remote(ref, ref, own_s.at[0, 0], own_r, sibling).wait_recv()

        @pl.when(jnp.logical_not(alone))
        def _():
            ref = view(16)
            remote(ref, ref, own_s.at[0, 0], own_r, sibling).wait_recv()

    def factor():
        panel_half(0)
        compute(1)
        below()
        panel_rest(0)
        for i in range(4):
            for k in range(i, 4):
                s = 0.5 * (blk(0, i, k) + blk(0, k, i).T)
                if i == k:
                    s = s + diag(i)
                x_ref[i * 128:i * 128 + 128, k * 128:k * 128 + 128] = s
            x_ref[i * 128:i * 128 + 128, 512:640] = blk(0, kr, i).T + jnp.where(kr == i, 1.0, 0.0) * diag(i)
        inverses = []
        for n in range(4):
            lo, hi = n * 128, n * 128 + 128
            width = 640 if n < 2 else NA
            ud, li = diag_factor(x_ref[lo:hi, lo:hi])
            inverses.append(li)
            if n == 2:
                panel_rest(1)
                for k in range(4):
                    x_ref[k * 128:k * 128 + 128, 640:768] = blk(1, kr, k).T
                    x_ref[k * 128:k * 128 + 128, 768:896] = blk(1, kc, k).T
                for k in range(2):
                    rows, later = slice(k * 128, k * 128 + 128), slice(k * 128 + 128, 512)
                    u = fdot(inverses[k], x_ref[rows, 640:NA])
                    x_ref[rows, 640:NA] = u
                    x_ref[later, 640:NA] = x_ref[later, 640:NA] - tdot(x_ref[rows, later], u)
            u = fdot(li, x_ref[lo:hi, hi:width])
            x_ref[lo:hi, hi:width] = u
            for nxt in range(n + 1, 4):
                c = nxt * 128
                x_ref[c:c + 128, c:width] = x_ref[c:c + 128, c:width] - tdot(u[:, c - hi:c - hi + 128], u[:, c - hi:])
            if n == 0:
                panel_sent(1)
                send_w2(1)
                compute(3)
                send_w2(3)
            if n == 1:
                panel_half(1)
                others(2)
            if n == 2:
                others(1)
                others(3)
            if n == 3:
                pass
        at = pl.multiple_of(kc * 128, 128)
        out[0:128, 0:128] = x_ref[pl.ds(at, 128), 512:640].T
        out[256:384, 0:128] = x_ref[pl.ds(at, 128), 640:768].T
        left = tdot(x_ref[:, 640:768], x_ref[:, 768:896])
        own_wait(lambda n: own.at[0:n, 2])
        out[256:384, 128:256] = mine(1, 1) - left

    for i in range(5):
        loads[i].wait()
    prepare(0)
    pl.semaphore_wait(barrier, 37)
    send_w1(0)
    for s in range(1, 4):
        loads[s + 4].wait()
        prepare(s)
        if s in (1, 2):
            send_w1(s)
    loads[8].wait()
    out[...] = jnp.zeros_like(out)
    forward(0)
    send_w1(3)
    compute(0)
    leading_start()
    multiply(0, 1)
    leading()
    forward(1)
    forward(2)
    panel_sent(0)
    below_start()
    compute(2)
    send_w2(2)
    forward(3)

    first_owner = (cls == 0) & (zh == 0)
    pl.when(first_owner)(factor)

    @pl.when(jnp.logical_not(first_owner))
    def _():
        compute(1)
        below()
        panel_sent(1)
        send_w2(1)
        compute(3)
        send_w2(3)
        others(2)
        others(1)
        others(3)

    @pl.when((cls > 0) & (zh == xh))
    def _():
        own_wait(lambda n: own.at[0:n])
        for t in range(2):
            at = pl.multiple_of((cls // 2 + 2 * t) * 128, 128)
            for u in range(2):
                out[pl.ds(at, 128), u * 128:u * 128 + 128] = mine(t, u)

    sent()


def body(col_data, col_scale, row_ids, live_rows, live_blocks, row_reg):
    anywhere = pl.BlockSpec(memory_space=pltpu.HBM)
    dma = pltpu.SemaphoreType.DMA
    return pl.pallas_call(
        kernel,
        out_shape=jax.ShapeDtypeStruct((512, 256), jnp.float32),
        in_specs=[anywhere] * 6,
        out_specs=pl.BlockSpec(memory_space=pltpu.VMEM),
        scratch_shapes=[
            pltpu.VMEM((4, 4, 128, 128), jnp.bfloat16),
            pltpu.VMEM((4, 128), jnp.bfloat16),
            pltpu.SMEM((4, 4), jnp.int32),
            pltpu.SMEM((4,), jnp.int32),
            pltpu.SMEM((1,), jnp.int32),
            pltpu.VMEM((32, 128), jnp.float32),
            pltpu.VMEM((16, 4, 8, 128), jnp.float32),
            pltpu.VMEM((2, 2, 2, 2, 16, 2, 8, 128), jnp.float32),
            pltpu.VMEM((4, 8, ROWS, 128), jnp.bfloat16),
            pltpu.VMEM((512, 1024), jnp.bfloat16),
            pltpu.VMEM((256, 1024), jnp.bfloat16),
            pltpu.VMEM((4, 16, 4, 2, 8, 128), jnp.float32),
            pltpu.VMEM((16, 1, 2, 8, 128), jnp.float32),
            pltpu.VMEM((16, 2, 2, 8, 128), jnp.float32),
            pltpu.VMEM((3, 16, 4, 2, 8, 128), jnp.float32),
            pltpu.VMEM((4, 4, 2, 8, 128), jnp.float32),
            pltpu.VMEM((512, NA), jnp.float32),
            dma((9,)),
            dma((4,)), dma((4,)), dma((4, 8)), dma((5,)), dma((5,)), dma((2,)), dma((2,)),
            dma((4, 2)), dma, dma((2,)), dma((2,)),
        ],
        compiler_params=pltpu.CompilerParams(
            collective_id=0, has_side_effects=True, vmem_limit_bytes=60 * 1024 * 1024),
    )(col_data, col_scale, row_ids, live_rows, live_blocks, row_reg.reshape(32, 128))


def solution(mesh):
    return jax.shard_map(
        body,
        mesh=mesh,
        in_specs=(
            P(("row", "col"), None, None, None),
            P(("row", "col"), None),
            P(("row", "col"), None),
            P(("row", "col")),
            P(("row", "col")),
            P(),
        ),
        out_specs=P("row", "col"),
        check_vma=False,
    )
```

```python
import jax
import jax.numpy as jnp
from jax import lax
from jax.experimental import pallas as pl
from jax.experimental.pallas import tpu as pltpu
from jax.sharding import PartitionSpec as P

HI = lax.Precision.HIGHEST
NA = 896
ROWS = 528
MESH = pl.DeviceIdType.MESH


def tdot(a, b):
    return lax.dot_general(a, b, (((0,), (0,)), ((), ())), precision=HI,
                           preferred_element_type=jnp.float32)


def fdot(a, b):
    return jnp.dot(a, b, precision=HI, preferred_element_type=jnp.float32)


def lanes(v):
    return jnp.broadcast_to(v, (v.shape[0], 128))


def diag_factor(d):
    row8 = lax.broadcasted_iota(jnp.int32, (8, 128), 0)
    e = jnp.where(lax.broadcasted_iota(jnp.int32, (128, 128), 0) == lax.broadcasted_iota(jnp.int32, (128, 128), 1), 1.0, 0.0)
    us, es = [], []
    for h in range(4):
        x, y = d[:32], e[:32]
        done_x, done_y = [], []
        for j in range(4):
            lane = 32 * h + 8 * j
            rows = 32 - 8 * j
            row = lax.broadcasted_iota(jnp.int32, (rows, 128), 0)
            cs = [lanes(x[:, lane + i:lane + i + 1]) for i in range(8)]
            scale = jnp.zeros((8, 128), jnp.float32)
            for i in range(0, 8, 2):
                a, b, c = cs[i][i:i + 1, :], cs[i + 1][i:i + 1, :], cs[i + 1][i + 1:i + 2, :]
                det = a * c - b * b
                ra, rdet = 1.0 / a, 1.0 / det
                w = b * ra
                scale = jnp.where(row8 == i, lax.rsqrt(a), scale)
                scale = jnp.where(row8 == i + 1, lax.rsqrt(det * ra), scale)
                f = jnp.where(row > i, cs[i] * ra, 0.0)
                g = jnp.where(row > i + 1, (cs[i + 1] - cs[i] * w) * (a * rdet), 0.0)
                for m in range(i + 2, 8):
                    t = cs[m][i:i + 1, :]
                    cs[m] = cs[m] - f * t - g * (cs[m][i + 1:i + 2, :] - w * t)
                t = x[i:i + 1, :]
                x = x - f * t - g * (x[i + 1:i + 2, :] - w * t)
                t = y[i:i + 1, :]
                y = y - f * t - g * (y[i + 1:i + 2, :] - w * t)
            done_x.append(x[:8] * scale)
            done_y.append(y[:8] * scale)
            x, y = x[8:], y[8:]
        ux = jnp.concatenate(done_x, axis=0)
        uy = jnp.concatenate(done_y, axis=0)
        us.append(ux)
        es.append(uy)
        if h < 3:
            both = fdot(ux.T[32 * (h + 1):], jnp.concatenate([ux, uy], axis=1))
            d = d[32:] - both[:, :128]
            e = e[32:] - both[:, 128:]
    return jnp.concatenate(us, axis=0), jnp.concatenate(es, axis=0)


def kernel(data_h, scale_h, ids_h, live_rows_h, live_blocks_h, reg_h, out,
           data, scale, ids, live_rows, live_blocks, reg, own, panel,
           gat, lbuf, rbuf, part, land0, land1, land, res, x_ref,
           ins, w1s, w1f, w1r, w2s, w2r, ps, pr, own_s, own_r, sib_s, sib_r):
    loads = [pltpu.make_async_copy(a, b, ins.at[i]) for i, (a, b) in enumerate((
        (ids_h, ids), (live_rows_h, live_rows), (live_blocks_h, live_blocks), (scale_h, scale),
        (data_h.at[0], data.at[0]), (data_h.at[1], data.at[1]), (data_h.at[2], data.at[2]),
        (data_h.at[3], data.at[3]), (reg_h, reg)))]
    r = lax.axis_index("row")
    q = lax.axis_index("col")
    z, yh = r // 2, lax.rem(r, 2)
    zh, zl = z // 2, lax.rem(z, 2)
    yl = q // 8
    x, e = lax.rem(q, 8) // 2, lax.rem(q, 2)
    xh, xl = x // 2, lax.rem(x, 2)
    y = 2 * yh + yl
    cls = 2 * yl + xh
    kr, kc = 2 * zl + yh, 2 * xl + e
    sibling = (r, q + 1 - 2 * e)
    order = ((0, 3), (1, 2))
    steps = ((2, 2), (1, 2), (3, 2), (2, 1), (2, 3), (0, 2), (2, 0), (1, 1), (3, 3), (1, 3), (3, 1), (0, 1), (0, 3), (1, 0), (3, 0))
    along = (x, y, z, z)
    place = (4 * z + y, 4 * z + x, 4 * y + x, 4 * y + x)

    def device(xx, yy, zz):
        return (2 * zz + yy // 2, lax.rem(yy, 2) * 8 + 2 * xx + e)

    def ring(s, d):
        u = lax.rem(along[s] + d, 4)
        to = (device(u, y, z), device(x, u, z), device(x, y, u), device(x, y, u))[s]
        return to, 2 * u + e

    def plane(s, p):
        a, b = p // 4, lax.rem(p, 4)
        return (device(x, b, a), device(b, y, a), device(b, a, z), device(b, a, z))[s]

    def remote(src, dst, send, recv, to):
        return pltpu.make_async_remote_copy(src_ref=src, dst_ref=dst, send_sem=send, recv_sem=recv,
                                            device_id=to, device_id_type=MESH)

    barrier = pltpu.get_barrier_semaphore()
    pl.semaphore_signal(barrier, inc=1, device_id=sibling, device_id_type=MESH)
    for dx in range(4):
        for dy in range(4):
            for dz in range(4):
                if 0 < (dx > 0) + (dy > 0) + (dz > 0) < 3:
                    to = device(lax.rem(x + dx, 4), lax.rem(y + dy, 4), lax.rem(z + dz, 4))
                    pl.semaphore_signal(barrier, inc=1, device_id=to, device_id_type=MESH)

    for load in loads:
        load.start()

    def prepare(s):
        j = 2 * along[s] + e
        row = lax.broadcasted_iota(jnp.int32, (16, 128), 0)
        on = s < live_blocks[0]
        meta = jnp.where(row == 0, jnp.broadcast_to(scale[...].astype(jnp.float32)[s:s + 1, :], (16, 128)), 0.0)
        for k in range(4):
            keep = jnp.where(on & (k < live_rows[s]), 1.0, 0.0)
            gat[s, j, k * 128:k * 128 + 128, :] = (data[s, k].astype(jnp.float32) * keep).astype(jnp.bfloat16)
            late = jnp.where(ids[s, k] >= 16, 1.0, 0.0)
            meta = jnp.where(row == k + 1, late, meta)
        gat[s, j, 512:528, :] = meta.astype(jnp.bfloat16)

    def send_w1(s):
        j = 2 * along[s] + e
        for d in (1, 3, 2, 0):
            remote(gat.at[s, j], gat.at[s, j], w1s.at[s], w1r.at[s, j], sibling if d == 0 else ring(s, d)[0]).start()

    def w1_arrived(s, j2):
        remote(gat.at[s, j2], gat.at[s, j2], w1f.at[s], w1r.at[s, j2], sibling).wait_recv()

    def forward(s):
        for d in (1, 3, 2):
            j2 = ring(s, d)[1]
            w1_arrived(s, j2)
            remote(gat.at[s, j2], gat.at[s, j2], w1f.at[s], w1r.at[s, j2], sibling).start()

    def compute(s):
        u = along[s]
        uh, ul = u // 2, lax.rem(u, 2)
        for d in (0, 1, 3, 2):
            w1_arrived(s, 2 * lax.rem(u + d, 4) + 1 - e)

        def build(c, _):
            meta = gat[s, c, 512:528, :].astype(jnp.float32)
            sc = meta[0:1, :]
            at = pl.multiple_of(c * 128, 128)
            for k in range(2):
                t = jnp.where(uh == 0, meta[1 + k:2 + k, :], meta[3 + k:4 + k, :])
                a = gat[s, c, pl.ds(pl.multiple_of((2 * uh + k) * 128, 128), 128), :].astype(jnp.float32)
                g = (a * sc).astype(jnp.bfloat16).astype(jnp.float32)
                lbuf[2 * k * 128:2 * k * 128 + 128, pl.ds(at, 128)] = (g * (1.0 - t)).astype(jnp.bfloat16)
                lbuf[2 * k * 128 + 128:2 * k * 128 + 256, pl.ds(at, 128)] = (g * t).astype(jnp.bfloat16)
            t0 = jnp.where(e == 0, meta[1:2, :], meta[2:3, :])
            t1 = jnp.where(e == 0, meta[3:4, :], meta[4:5, :])
            t = jnp.where(ul == 0, t0, t1)
            a = gat[s, c, pl.ds(pl.multiple_of((2 * ul + e) * 128, 128), 128), :].astype(jnp.float32)
            rbuf[0:128, pl.ds(at, 128)] = (a * (1.0 - t)).astype(jnp.bfloat16)
            rbuf[128:256, pl.ds(at, 128)] = (a * t).astype(jnp.bfloat16)
            return 0

        lax.fori_loop(0, 8, build, 0)
        multiply(s, 0)
        if s > 0:
            multiply(s, 1)

    def multiply(s, t):
        for k in range(2):
            row = (2 * k + t) * 128
            acc = lax.dot_general(lbuf[row:row + 128, :], rbuf[...], (((1,), (1,)), ((), ())),
                                  preferred_element_type=jnp.float32)
            for u in range(2):
                part[s, :, order[t][u], k] = acc[:, u * 128:u * 128 + 128].reshape(16, 8, 128)

    def w2(s, d, first, count, to_buf, sem):
        da, db = steps[d - 1]
        to = 4 * lax.rem(place[s] // 4 + da, 4) + lax.rem(place[s] + db, 4)
        return remote(part.at[s, to, first:first + count], to_buf.at[place[s]], w2s.at[sem], w2r.at[sem], plane(s, to))

    def w2_wait(buf, sem):
        remote(buf.at[0:15], buf.at[0:15], w2s.at[sem], w2r.at[sem], sibling).wait_recv()

    def w2_sum(s, mine, buf):
        total = mine
        for d in range(1, 16):
            total = total + buf[lax.rem(place[s] + d, 16)]
        return total

    def owner_of(s, k):
        uh, ul = along[s] // 2, lax.rem(along[s], 2)
        to = device(2 * (s % 2) + ul, 2 * k + s // 2, 2 * (s % 2) + uh)
        return to, (to[0] != r) | (to[1] != q)

    def to_panel(t):
        for d in range(8):
            to = ((d // 4) * 2 + (d // 2) % 2, (d % 2) * 2 + 1 - e)
            remote(res.at[0, t], panel.at[e, t, xl, xh, place[0]], ps.at[t], pr.at[t], to).start()

    def panel_sent(t):
        remote(land0.at[0:8], land0.at[0:8], ps.at[t], pr.at[t], sibling).wait_send()

    def leading_start():
        for d in range(1, 16):
            w2(0, d, 0, 1, land0, 0).start()

    def leading():
        w2_wait(land0, 0)
        res[0, 0:1] = w2_sum(0, part[0, place[0], 0:1], land0)
        to_panel(0)

    def below_start():
        for d in range(1, 16):
            w2(0, d, 1, 2, land1, 1).start()

    def below():
        w2_wait(land1, 1)
        res[0, 1:3] = w2_sum(0, part[0, place[0], 1:3], land1)
        to_panel(1)
        for k in range(2):
            to, away = owner_of(0, k)
            pl.when(away)(remote(res.at[0, 2, k], own.at[place[0], 2], own_s.at[0, k], own_r, to).start)

            @pl.when(jnp.logical_not(away))
            def _():
                own[place[0], 2] = res[0, 2, k]

    def send_w2(s):
        for d in range(1, 16):
            w2(s, d, 0, 4, land.at[s - 1], s + 1).start()

    def others(s):
        w2_wait(land.at[s - 1], s + 1)
        res[s] = w2_sum(s, part[s, place[s]], land.at[s - 1])
        for k in range(2):
            to, away = owner_of(s, k)
            pl.when(away)(remote(res.at[s, :, k], own.at[place[s]], own_s.at[s, k], own_r, to).start)

            @pl.when(jnp.logical_not(away))
            def _():
                own[place[s]] = res[s, :, k]

    def sent():
        def one(s, _):
            remote(gat.at[s, 0:4], gat.at[s, 0:4], w1s.at[s], w1r.at[s, 0], sibling).wait_send()
            remote(gat.at[s, 0:3], gat.at[s, 0:3], w1f.at[s], w1r.at[s, 0], sibling).wait_send()
            return 0

        lax.fori_loop(0, 4, one, 0)
        for buf, sem in ((land0, 0), (land1, 1), (land.at[0], 2), (land.at[1], 3), (land.at[2], 4)):
            remote(buf.at[0:15], buf.at[0:15], w2s.at[sem], w2r.at[sem], sibling).wait_send()
        for k in range(2):
            to, away = owner_of(0, k)
            pl.when(away)(remote(res.at[0, 2, k], own.at[place[0], 2], own_s.at[0, k], own_r, to).wait_send)
        for s in range(1, 4):
            for k in range(2):
                to, away = owner_of(s, k)
                pl.when(away)(remote(res.at[s, :, k], own.at[place[s]], own_s.at[s, k], own_r, to).wait_send)

    eye = (lax.broadcasted_iota(jnp.int32, (128, 128), 0) == lax.broadcasted_iota(jnp.int32, (128, 128), 1))

    def diag(block):
        return jnp.where(eye, jnp.broadcast_to(reg[pl.ds(block, 1), :], (128, 128)), 0.0)

    def blk(t, a, b):
        return panel[b % 2 if isinstance(b, int) else lax.rem(b, 2), t, b // 2, a // 2, :,
                     a % 2 if isinstance(a, int) else lax.rem(a, 2)].reshape(128, 128)

    def mine(t, u):
        base = own[:, order[t][u]].reshape(128, 128)
        if t == u:
            base = base + jnp.where(kr == kc, 1.0, 0.0) * diag(cls * 4 + kr + 16 * t)
        return base

    def panel_half(t):
        remote(panel.at[1 - e, t], panel.at[1 - e, t], ps.at[t], pr.at[t], sibling).wait_recv()
        remote(panel.at[1 - e, t], panel.at[1 - e, t], sib_s.at[t], sib_r.at[t], sibling).start()

    def panel_rest(t):
        copy = remote(panel.at[1 - e, t], panel.at[e, t], sib_s.at[t], sib_r.at[t], sibling)
        copy.wait_recv()
        copy.wait_send()

    def own_wait(view):
        mark = 2 * zl + xl
        alone = ((cls == 0) & (x == mark)) | ((cls == 1) & (y == mark)) | ((cls > 1) & (z == mark))

        @pl.when(alone)
        def _():
            ref = view(15)
            remote(ref, ref, own_s.at[0, 0], own_r, sibling).wait_recv()

        @pl.when(jnp.logical_not(alone))
        def _():
            ref = view(16)
            remote(ref, ref, own_s.at[0, 0], own_r, sibling).wait_recv()

    def factor():
        panel_half(0)
        compute(1)
        below()
        panel_rest(0)
        for i in range(4):
            for k in range(i, 4):
                s = 0.5 * (blk(0, i, k) + blk(0, k, i).T)
                if i == k:
                    s = s + diag(i)
                x_ref[i * 128:i * 128 + 128, k * 128:k * 128 + 128] = s
            x_ref[i * 128:i * 128 + 128, 512:640] = blk(0, kr, i).T + jnp.where(kr == i, 1.0, 0.0) * diag(i)
        inverses = []
        for n in range(4):
            lo, hi = n * 128, n * 128 + 128
            width = 640 if n < 2 else NA
            ud, li = diag_factor(x_ref[lo:hi, lo:hi])
            inverses.append(li)
            if n == 2:
                others(1)
                others(3)
                panel_rest(1)
                for k in range(4):
                    x_ref[k * 128:k * 128 + 128, 640:768] = blk(1, kr, k).T
                    x_ref[k * 128:k * 128 + 128, 768:896] = blk(1, kc, k).T
                for k in range(2):
                    rows, later = slice(k * 128, k * 128 + 128), slice(k * 128 + 128, 512)
                    u = fdot(inverses[k], x_ref[rows, 640:NA])
                    x_ref[rows, 640:NA] = u
                    x_ref[later, 640:NA] = x_ref[later, 640:NA] - tdot(x_ref[rows, later], u)
            u = fdot(li, x_ref[lo:hi, hi:width])
            x_ref[lo:hi, hi:width] = u
            for nxt in range(n + 1, 4):
                c = nxt * 128
                x_ref[c:c + 128, c:width] = x_ref[c:c + 128, c:width] - tdot(u[:, c - hi:c - hi + 128], u[:, c - hi:])
            if n == 0:
                panel_sent(1)
                send_w2(1)
                compute(3)
                send_w2(3)
            if n == 1:
                panel_half(1)
                others(2)
            if n == 3:
                pass
        at = pl.multiple_of(kc * 128, 128)
        out[0:128, 0:128] = x_ref[pl.ds(at, 128), 512:640].T
        out[256:384, 0:128] = x_ref[pl.ds(at, 128), 640:768].T
        left = tdot(x_ref[:, 640:768], x_ref[:, 768:896])
        own_wait(lambda n: own.at[0:n, 2])
        out[256:384, 128:256] = mine(1, 1) - left

    for i in range(5):
        loads[i].wait()
    prepare(0)
    pl.semaphore_wait(barrier, 37)
    send_w1(0)
    for s in range(1, 4):
        loads[s + 4].wait()
        prepare(s)
        if s in (1, 2):
            send_w1(s)
    loads[8].wait()
    out[...] = jnp.zeros_like(out)
    forward(0)
    send_w1(3)
    compute(0)
    leading_start()
    multiply(0, 1)
    leading()
    forward(1)
    forward(2)
    panel_sent(0)
    below_start()
    compute(2)
    send_w2(2)
    forward(3)

    first_owner = (cls == 0) & (zh == 0)
    pl.when(first_owner)(factor)

    @pl.when(jnp.logical_not(first_owner))
    def _():
        compute(1)
        below()
        panel_sent(1)
        send_w2(1)
        compute(3)
        send_w2(3)
        others(2)
        others(1)
        others(3)

    @pl.when((cls > 0) & (zh == xh))
    def _():
        own_wait(lambda n: own.at[0:n])
        for t in range(2):
            at = pl.multiple_of((cls // 2 + 2 * t) * 128, 128)
            for u in range(2):
                out[pl.ds(at, 128), u * 128:u * 128 + 128] = mine(t, u)

    sent()


def body(col_data, col_scale, row_ids, live_rows, live_blocks, row_reg):
    anywhere = pl.BlockSpec(memory_space=pltpu.HBM)
    dma = pltpu.SemaphoreType.DMA
    return pl.pallas_call(
        kernel,
        out_shape=jax.ShapeDtypeStruct((512, 256), jnp.float32),
        in_specs=[anywhere] * 6,
        out_specs=pl.BlockSpec(memory_space=pltpu.VMEM),
        scratch_shapes=[
            pltpu.VMEM((4, 4, 128, 128), jnp.bfloat16),
            pltpu.VMEM((4, 128), jnp.bfloat16),
            pltpu.SMEM((4, 4), jnp.int32),
            pltpu.SMEM((4,), jnp.int32),
            pltpu.SMEM((1,), jnp.int32),
            pltpu.VMEM((32, 128), jnp.float32),
            pltpu.VMEM((16, 4, 8, 128), jnp.float32),
            pltpu.VMEM((2, 2, 2, 2, 16, 2, 8, 128), jnp.float32),
            pltpu.VMEM((4, 8, ROWS, 128), jnp.bfloat16),
            pltpu.VMEM((512, 1024), jnp.bfloat16),
            pltpu.VMEM((256, 1024), jnp.bfloat16),
            pltpu.VMEM((4, 16, 4, 2, 8, 128), jnp.float32),
            pltpu.VMEM((16, 1, 2, 8, 128), jnp.float32),
            pltpu.VMEM((16, 2, 2, 8, 128), jnp.float32),
            pltpu.VMEM((3, 16, 4, 2, 8, 128), jnp.float32),
            pltpu.VMEM((4, 4, 2, 8, 128), jnp.float32),
            pltpu.VMEM((512, NA), jnp.float32),
            dma((9,)),
            dma((4,)), dma((4,)), dma((4, 8)), dma((5,)), dma((5,)), dma((2,)), dma((2,)),
            dma((4, 2)), dma, dma((2,)), dma((2,)),
        ],
        compiler_params=pltpu.CompilerParams(
            collective_id=0, has_side_effects=True, vmem_limit_bytes=60 * 1024 * 1024),
    )(col_data, col_scale, row_ids, live_rows, live_blocks, row_reg.reshape(32, 128))


def solution(mesh):
    return jax.shard_map(
        body,
        mesh=mesh,
        in_specs=(
            P(("row", "col"), None, None, None),
            P(("row", "col"), None),
            P(("row", "col"), None),
            P(("row", "col")),
            P(("row", "col")),
            P(),
        ),
        out_specs=P("row", "col"),
        check_vma=False,
    )
```

```python
import jax
import jax.numpy as jnp
from jax import lax
from jax.experimental import pallas as pl
from jax.experimental.pallas import tpu as pltpu
from jax.sharding import PartitionSpec as P

HI = lax.Precision.HIGHEST
NA = 896
ROWS = 528
MESH = pl.DeviceIdType.MESH


def tdot(a, b):
    return lax.dot_general(a, b, (((0,), (0,)), ((), ())), precision=HI,
                           preferred_element_type=jnp.float32)


def fdot(a, b):
    return jnp.dot(a, b, precision=HI, preferred_element_type=jnp.float32)


def lanes(v):
    return jnp.broadcast_to(v, (v.shape[0], 128))


def diag_factor(d):
    row8 = lax.broadcasted_iota(jnp.int32, (8, 128), 0)
    e = jnp.where(lax.broadcasted_iota(jnp.int32, (128, 128), 0) == lax.broadcasted_iota(jnp.int32, (128, 128), 1), 1.0, 0.0)
    us, es = [], []
    for h in range(4):
        x, y = d[:32], e[:32]
        done_x, done_y = [], []
        for j in range(4):
            lane = 32 * h + 8 * j
            rows = 32 - 8 * j
            row = lax.broadcasted_iota(jnp.int32, (rows, 128), 0)
            cs = [lanes(x[:, lane + i:lane + i + 1]) for i in range(8)]
            scale = jnp.zeros((8, 128), jnp.float32)
            for i in range(0, 8, 2):
                a, b, c = cs[i][i:i + 1, :], cs[i + 1][i:i + 1, :], cs[i + 1][i + 1:i + 2, :]
                det = a * c - b * b
                ra, rdet = 1.0 / a, 1.0 / det
                w = b * ra
                scale = jnp.where(row8 == i, lax.rsqrt(a), scale)
                scale = jnp.where(row8 == i + 1, lax.rsqrt(det * ra), scale)
                f = jnp.where(row > i, cs[i] * ra, 0.0)
                g = jnp.where(row > i + 1, (cs[i + 1] - cs[i] * w) * (a * rdet), 0.0)
                for m in range(i + 2, 8):
                    t = cs[m][i:i + 1, :]
                    cs[m] = cs[m] - f * t - g * (cs[m][i + 1:i + 2, :] - w * t)
                t = x[i:i + 1, :]
                x = x - f * t - g * (x[i + 1:i + 2, :] - w * t)
                t = y[i:i + 1, :]
                y = y - f * t - g * (y[i + 1:i + 2, :] - w * t)
            done_x.append(x[:8] * scale)
            done_y.append(y[:8] * scale)
            x, y = x[8:], y[8:]
        ux = jnp.concatenate(done_x, axis=0)
        uy = jnp.concatenate(done_y, axis=0)
        us.append(ux)
        es.append(uy)
        if h < 3:
            both = fdot(ux.T[32 * (h + 1):], jnp.concatenate([ux, uy], axis=1))
            d = d[32:] - both[:, :128]
            e = e[32:] - both[:, 128:]
    return jnp.concatenate(us, axis=0), jnp.concatenate(es, axis=0)


def kernel(data_h, scale_h, ids_h, live_rows_h, live_blocks_h, reg_h, out,
           data, scale, ids, live_rows, live_blocks, reg, own, panel,
           gat, lbuf, rbuf, part, land0, land1, land, res, x_ref,
           ins, w1s, w1f, w1r, w2s, w2r, ps, pr, own_s, own_r, sib_s, sib_r):
    loads = [pltpu.make_async_copy(a, b, ins.at[i]) for i, (a, b) in enumerate((
        (ids_h, ids), (live_rows_h, live_rows), (live_blocks_h, live_blocks), (scale_h, scale),
        (data_h.at[0], data.at[0]), (data_h.at[1], data.at[1]), (data_h.at[2], data.at[2]),
        (data_h.at[3], data.at[3]), (reg_h, reg)))]
    r = lax.axis_index("row")
    q = lax.axis_index("col")
    z, yh = r // 2, lax.rem(r, 2)
    zh, zl = z // 2, lax.rem(z, 2)
    yl = q // 8
    x, e = lax.rem(q, 8) // 2, lax.rem(q, 2)
    xh, xl = x // 2, lax.rem(x, 2)
    y = 2 * yh + yl
    cls = 2 * yl + xh
    kr, kc = 2 * zl + yh, 2 * xl + e
    sibling = (r, q + 1 - 2 * e)
    order = ((0, 3), (1, 2))
    steps = ((2, 2), (1, 2), (3, 2), (2, 1), (2, 3), (0, 2), (2, 0), (1, 1), (3, 3), (1, 3), (3, 1), (0, 1), (0, 3), (1, 0), (3, 0))
    along = (x, y, z, z)
    place = (4 * z + y, 4 * z + x, 4 * y + x, 4 * y + x)

    def device(xx, yy, zz):
        return (2 * zz + yy // 2, lax.rem(yy, 2) * 8 + 2 * xx + e)

    def ring(s, d):
        u = lax.rem(along[s] + d, 4)
        to = (device(u, y, z), device(x, u, z), device(x, y, u), device(x, y, u))[s]
        return to, 2 * u + e

    def plane(s, p):
        a, b = p // 4, lax.rem(p, 4)
        return (device(x, b, a), device(b, y, a), device(b, a, z), device(b, a, z))[s]

    def remote(src, dst, send, recv, to):
        return pltpu.make_async_remote_copy(src_ref=src, dst_ref=dst, send_sem=send, recv_sem=recv,
                                            device_id=to, device_id_type=MESH)

    barrier = pltpu.get_barrier_semaphore()
    pl.semaphore_signal(barrier, inc=1, device_id=sibling, device_id_type=MESH)
    for dx in range(4):
        for dy in range(4):
            for dz in range(4):
                if 0 < (dx > 0) + (dy > 0) + (dz > 0) < 3:
                    to = device(lax.rem(x + dx, 4), lax.rem(y + dy, 4), lax.rem(z + dz, 4))
                    pl.semaphore_signal(barrier, inc=1, device_id=to, device_id_type=MESH)

    for load in loads:
        load.start()

    def prepare(s):
        j = 2 * along[s] + e
        row = lax.broadcasted_iota(jnp.int32, (16, 128), 0)
        on = s < live_blocks[0]
        meta = jnp.where(row == 0, jnp.broadcast_to(scale[...].astype(jnp.float32)[s:s + 1, :], (16, 128)), 0.0)
        for k in range(4):
            keep = jnp.where(on & (k < live_rows[s]), 1.0, 0.0)
            gat[s, j, k * 128:k * 128 + 128, :] = (data[s, k].astype(jnp.float32) * keep).astype(jnp.bfloat16)
            late = jnp.where(ids[s, k] >= 16, 1.0, 0.0)
            meta = jnp.where(row == k + 1, late, meta)
        gat[s, j, 512:528, :] = meta.astype(jnp.bfloat16)

    def send_w1(s):
        j = 2 * along[s] + e
        for d in (1, 3, 2, 0):
            remote(gat.at[s, j], gat.at[s, j], w1s.at[s], w1r.at[s, j], sibling if d == 0 else ring(s, d)[0]).start()

    def w1_arrived(s, j2):
        remote(gat.at[s, j2], gat.at[s, j2], w1f.at[s], w1r.at[s, j2], sibling).wait_recv()

    def forward(s):
        for d in (1, 3, 2):
            j2 = ring(s, d)[1]
            w1_arrived(s, j2)
            remote(gat.at[s, j2], gat.at[s, j2], w1f.at[s], w1r.at[s, j2], sibling).start()

    def compute(s):
        u = along[s]
        uh, ul = u // 2, lax.rem(u, 2)
        for d in (0, 1, 3, 2):
            w1_arrived(s, 2 * lax.rem(u + d, 4) + 1 - e)

        def build(c, _):
            meta = gat[s, c, 512:528, :].astype(jnp.float32)
            sc = meta[0:1, :]
            at = pl.multiple_of(c * 128, 128)
            for k in range(2):
                t = jnp.where(uh == 0, meta[1 + k:2 + k, :], meta[3 + k:4 + k, :])
                a = gat[s, c, pl.ds(pl.multiple_of((2 * uh + k) * 128, 128), 128), :].astype(jnp.float32)
                g = (a * sc).astype(jnp.bfloat16).astype(jnp.float32)
                lbuf[2 * k * 128:2 * k * 128 + 128, pl.ds(at, 128)] = (g * (1.0 - t)).astype(jnp.bfloat16)
                lbuf[2 * k * 128 + 128:2 * k * 128 + 256, pl.ds(at, 128)] = (g * t).astype(jnp.bfloat16)
            t0 = jnp.where(e == 0, meta[1:2, :], meta[2:3, :])
            t1 = jnp.where(e == 0, meta[3:4, :], meta[4:5, :])
            t = jnp.where(ul == 0, t0, t1)
            a = gat[s, c, pl.ds(pl.multiple_of((2 * ul + e) * 128, 128), 128), :].astype(jnp.float32)
            rbuf[0:128, pl.ds(at, 128)] = (a * (1.0 - t)).astype(jnp.bfloat16)
            rbuf[128:256, pl.ds(at, 128)] = (a * t).astype(jnp.bfloat16)
            return 0

        lax.fori_loop(0, 8, build, 0)
        multiply(s, 0)
        if s > 0:
            multiply(s, 1)

    def multiply(s, t):
        for k in range(2):
            row = (2 * k + t) * 128
            acc = lax.dot_general(lbuf[row:row + 128, :], rbuf[...], (((1,), (1,)), ((), ())),
                                  preferred_element_type=jnp.float32)
            for u in range(2):
                part[s, :, order[t][u], k] = acc[:, u * 128:u * 128 + 128].reshape(16, 8, 128)

    def w2(s, d, first, count, to_buf, sem):
        da, db = steps[d - 1]
        to = 4 * lax.rem(place[s] // 4 + da, 4) + lax.rem(place[s] + db, 4)
        return remote(part.at[s, to, first:first + count], to_buf.at[place[s]], w2s.at[sem], w2r.at[sem], plane(s, to))

    def w2_wait(buf, sem):
        remote(buf.at[0:15], buf.at[0:15], w2s.at[sem], w2r.at[sem], sibling).wait_recv()

    def w2_sum(s, mine, buf):
        total = mine
        for d in range(1, 16):
            total = total + buf[lax.rem(place[s] + d, 16)]
        return total

    def owner_of(s, k):
        uh, ul = along[s] // 2, lax.rem(along[s], 2)
        to = device(2 * (s % 2) + ul, 2 * k + s // 2, 2 * (s % 2) + uh)
        return to, (to[0] != r) | (to[1] != q)

    def to_panel(t):
        for d in range(8):
            c = lax.rem(place[0] + d, 8)
            to = ((c // 4) * 2 + lax.rem(c // 2, 2), lax.rem(c, 2) * 2 + 1 - e)
            remote(res.at[0, t], panel.at[e, t, xl, xh, place[0]], ps.at[t], pr.at[t], to).start()

    def panel_sent(t):
        remote(land0.at[0:8], land0.at[0:8], ps.at[t], pr.at[t], sibling).wait_send()

    def leading_start():
        for d in range(1, 16):
            w2(0, d, 0, 1, land0, 0).start()

    def leading():
        w2_wait(land0, 0)
        res[0, 0:1] = w2_sum(0, part[0, place[0], 0:1], land0)
        to_panel(0)

    def below_start():
        for d in range(1, 16):
            w2(0, d, 1, 2, land1, 1).start()

    def below():
        w2_wait(land1, 1)
        res[0, 1:3] = w2_sum(0, part[0, place[0], 1:3], land1)
        to_panel(1)
        for k in range(2):
            to, away = owner_of(0, k)
            pl.when(away)(remote(res.at[0, 2, k], own.at[place[0], 2], own_s.at[0, k], own_r, to).start)

            @pl.when(jnp.logical_not(away))
            def _():
                own[place[0], 2] = res[0, 2, k]

    def send_w2(s):
        for d in range(1, 16):
            w2(s, d, 0, 4, land.at[s - 1], s + 1).start()

    def others(s):
        w2_wait(land.at[s - 1], s + 1)
        res[s] = w2_sum(s, part[s, place[s]], land.at[s - 1])
        for k in range(2):
            to, away = owner_of(s, k)
            pl.when(away)(remote(res.at[s, :, k], own.at[place[s]], own_s.at[s, k], own_r, to).start)

            @pl.when(jnp.logical_not(away))
            def _():
                own[place[s]] = res[s, :, k]

    def sent():
        def one(s, _):
            remote(gat.at[s, 0:4], gat.at[s, 0:4], w1s.at[s], w1r.at[s, 0], sibling).wait_send()
            remote(gat.at[s, 0:3], gat.at[s, 0:3], w1f.at[s], w1r.at[s, 0], sibling).wait_send()
            return 0

        lax.fori_loop(0, 4, one, 0)
        for buf, sem in ((land0, 0), (land1, 1), (land.at[0], 2), (land.at[1], 3), (land.at[2], 4)):
            remote(buf.at[0:15], buf.at[0:15], w2s.at[sem], w2r.at[sem], sibling).wait_send()
        for k in range(2):
            to, away = owner_of(0, k)
            pl.when(away)(remote(res.at[0, 2, k], own.at[place[0], 2], own_s.at[0, k], own_r, to).wait_send)
        for s in range(1, 4):
            for k in range(2):
                to, away = owner_of(s, k)
                pl.when(away)(remote(res.at[s, :, k], own.at[place[s]], own_s.at[s, k], own_r, to).wait_send)

    eye = (lax.broadcasted_iota(jnp.int32, (128, 128), 0) == lax.broadcasted_iota(jnp.int32, (128, 128), 1))

    def diag(block):
        return jnp.where(eye, jnp.broadcast_to(reg[pl.ds(block, 1), :], (128, 128)), 0.0)

    def blk(t, a, b):
        return panel[b % 2 if isinstance(b, int) else lax.rem(b, 2), t, b // 2, a // 2, :,
                     a % 2 if isinstance(a, int) else lax.rem(a, 2)].reshape(128, 128)

    def mine(t, u):
        base = own[:, order[t][u]].reshape(128, 128)
        if t == u:
            base = base + jnp.where(kr == kc, 1.0, 0.0) * diag(cls * 4 + kr + 16 * t)
        return base

    def panel_half(t):
        remote(panel.at[1 - e, t], panel.at[1 - e, t], ps.at[t], pr.at[t], sibling).wait_recv()
        remote(panel.at[1 - e, t], panel.at[1 - e, t], sib_s.at[t], sib_r.at[t], sibling).start()

    def panel_rest(t):
        copy = remote(panel.at[1 - e, t], panel.at[e, t], sib_s.at[t], sib_r.at[t], sibling)
        copy.wait_recv()
        copy.wait_send()

    def own_wait(view):
        mark = 2 * zl + xl
        alone = ((cls == 0) & (x == mark)) | ((cls == 1) & (y == mark)) | ((cls > 1) & (z == mark))

        @pl.when(alone)
        def _():
            ref = view(15)
            remote(ref, ref, own_s.at[0, 0], own_r, sibling).wait_recv()

        @pl.when(jnp.logical_not(alone))
        def _():
            ref = view(16)
            remote(ref, ref, own_s.at[0, 0], own_r, sibling).wait_recv()

    def factor():
        panel_half(0)
        compute(1)
        below()
        panel_rest(0)
        for i in range(4):
            for k in range(i, 4):
                s = 0.5 * (blk(0, i, k) + blk(0, k, i).T)
                if i == k:
                    s = s + diag(i)
                x_ref[i * 128:i * 128 + 128, k * 128:k * 128 + 128] = s
            x_ref[i * 128:i * 128 + 128, 512:640] = blk(0, kr, i).T + jnp.where(kr == i, 1.0, 0.0) * diag(i)
        inverses = []
        for n in range(4):
            lo, hi = n * 128, n * 128 + 128
            width = 640 if n < 2 else NA
            ud, li = diag_factor(x_ref[lo:hi, lo:hi])
            inverses.append(li)
            if n == 2:
                others(1)
                others(3)
                panel_rest(1)
                for k in range(4):
                    x_ref[k * 128:k * 128 + 128, 640:768] = blk(1, kr, k).T
                    x_ref[k * 128:k * 128 + 128, 768:896] = blk(1, kc, k).T
                for k in range(2):
                    rows, later = slice(k * 128, k * 128 + 128), slice(k * 128 + 128, 512)
                    u = fdot(inverses[k], x_ref[rows, 640:NA])
                    x_ref[rows, 640:NA] = u
                    x_ref[later, 640:NA] = x_ref[later, 640:NA] - tdot(x_ref[rows, later], u)
            u = fdot(li, x_ref[lo:hi, hi:width])
            x_ref[lo:hi, hi:width] = u
            for nxt in range(n + 1, 4):
                c = nxt * 128
                x_ref[c:c + 128, c:width] = x_ref[c:c + 128, c:width] - tdot(u[:, c - hi:c - hi + 128], u[:, c - hi:])
            if n == 0:
                panel_sent(1)
                send_w2(1)
                compute(3)
                send_w2(3)
            if n == 1:
                panel_half(1)
                others(2)
            if n == 3:
                pass
        at = pl.multiple_of(kc * 128, 128)
        out[0:128, 0:128] = x_ref[pl.ds(at, 128), 512:640].T
        out[256:384, 0:128] = x_ref[pl.ds(at, 128), 640:768].T
        left = tdot(x_ref[:, 640:768], x_ref[:, 768:896])
        own_wait(lambda n: own.at[0:n, 2])
        out[256:384, 128:256] = mine(1, 1) - left

    for i in range(5):
        loads[i].wait()
    prepare(0)
    pl.semaphore_wait(barrier, 37)
    send_w1(0)
    for s in range(1, 4):
        loads[s + 4].wait()
        prepare(s)
        if s in (1, 2):
            send_w1(s)
    loads[8].wait()
    out[...] = jnp.zeros_like(out)
    forward(0)
    send_w1(3)
    compute(0)
    leading_start()
    multiply(0, 1)
    leading()
    forward(1)
    forward(2)
    panel_sent(0)
    below_start()
    compute(2)
    send_w2(2)
    forward(3)

    first_owner = (cls == 0) & (zh == 0)
    pl.when(first_owner)(factor)

    @pl.when(jnp.logical_not(first_owner))
    def _():
        compute(1)
        below()
        panel_sent(1)
        send_w2(1)
        compute(3)
        send_w2(3)
        others(2)
        others(1)
        others(3)

    @pl.when((cls > 0) & (zh == xh))
    def _():
        own_wait(lambda n: own.at[0:n])
        for t in range(2):
            at = pl.multiple_of((cls // 2 + 2 * t) * 128, 128)
            for u in range(2):
                out[pl.ds(at, 128), u * 128:u * 128 + 128] = mine(t, u)

    sent()


def body(col_data, col_scale, row_ids, live_rows, live_blocks, row_reg):
    anywhere = pl.BlockSpec(memory_space=pltpu.HBM)
    dma = pltpu.SemaphoreType.DMA
    return pl.pallas_call(
        kernel,
        out_shape=jax.ShapeDtypeStruct((512, 256), jnp.float32),
        in_specs=[anywhere] * 6,
        out_specs=pl.BlockSpec(memory_space=pltpu.VMEM),
        scratch_shapes=[
            pltpu.VMEM((4, 4, 128, 128), jnp.bfloat16),
            pltpu.VMEM((4, 128), jnp.bfloat16),
            pltpu.SMEM((4, 4), jnp.int32),
            pltpu.SMEM((4,), jnp.int32),
            pltpu.SMEM((1,), jnp.int32),
            pltpu.VMEM((32, 128), jnp.float32),
            pltpu.VMEM((16, 4, 8, 128), jnp.float32),
            pltpu.VMEM((2, 2, 2, 2, 16, 2, 8, 128), jnp.float32),
            pltpu.VMEM((4, 8, ROWS, 128), jnp.bfloat16),
            pltpu.VMEM((512, 1024), jnp.bfloat16),
            pltpu.VMEM((256, 1024), jnp.bfloat16),
            pltpu.VMEM((4, 16, 4, 2, 8, 128), jnp.float32),
            pltpu.VMEM((16, 1, 2, 8, 128), jnp.float32),
            pltpu.VMEM((16, 2, 2, 8, 128), jnp.float32),
            pltpu.VMEM((3, 16, 4, 2, 8, 128), jnp.float32),
            pltpu.VMEM((4, 4, 2, 8, 128), jnp.float32),
            pltpu.VMEM((512, NA), jnp.float32),
            dma((9,)),
            dma((4,)), dma((4,)), dma((4, 8)), dma((5,)), dma((5,)), dma((2,)), dma((2,)),
            dma((4, 2)), dma, dma((2,)), dma((2,)),
        ],
        compiler_params=pltpu.CompilerParams(
            collective_id=0, has_side_effects=True, vmem_limit_bytes=60 * 1024 * 1024),
    )(col_data, col_scale, row_ids, live_rows, live_blocks, row_reg.reshape(32, 128))


def solution(mesh):
    return jax.shard_map(
        body,
        mesh=mesh,
        in_specs=(
            P(("row", "col"), None, None, None),
            P(("row", "col"), None),
            P(("row", "col"), None),
            P(("row", "col")),
            P(("row", "col")),
            P(),
        ),
        out_specs=P("row", "col"),
        check_vma=False,
    )
```
